128 devices in a mesh: dp: 16 (over x_lo, z, core), tensor: 8 (over y, x_hi).
Axes of the slice: x: 4 (x_hi: 2, x_lo: 2; x = x_hi * 2 + x_lo), y: 4, z: 4, core: 2. Of those that a mesh axis runs over, the one named last changes fastest.
Arguments:
- tokens: bfloat16 [16384, 1024], P(('dp', 'tensor')), may hold values from -6 to 6
- lengths: int32 [16, 3], P('dp'), may hold values from 1 to 960, 1024 in all within a row
- qkv_weight: bfloat16 [2, 1024, 3, 1024], P(None, 'dp', None, 'tensor'), may hold values from -0.1875 to 0.1875
- qkv_bias: bfloat16 [2, 3, 1024], P(None, None, 'tensor'), may hold values from -3 to 3
- dense_weight: bfloat16 [2, 1024, 1024], P(None, 'tensor', 'dp'), may hold values from -0.75 to 0.75
- dense_bias: bfloat16 [2, 1024], replicated, may hold values from -2 to 2
- fc_in_weight: bfloat16 [2, 1024, 4096], P(None, 'dp', 'tensor'), may hold values from -0.1875 to 0.1875
- fc_in_bias: bfloat16 [2, 4096], P(None, 'tensor'), may hold values from -3 to 3
- fc_out_weight: bfloat16 [2, 4096, 1024], P(None, 'tensor', 'dp'), may hold values from -0.09375 to 0.09375
- fc_out_bias: bfloat16 [2, 1024], replicated, may hold values from -2 to 2
- norm_gain: bfloat16 [2, 2, 1024], replicated, may hold values from 0.5 to 1.5
- norm_bias: bfloat16 [2, 2, 1024], replicated, may hold values from -2 to 2
- cotangent: bfloat16 [16384, 1024], P(('dp', 'tensor')), may hold values from -6 to 6
Outputs:
- output: bfloat16 [16384, 1024], P(('dp', 'tensor'))
- input_grad: float32 [16384, 1024], P(('dp', 'tensor'))
- qkv_weight_grad: float32 [2, 1024, 3, 1024], P(None, 'dp', None, 'tensor')
- qkv_bias_grad: float32 [2, 3, 1024], P(None, None, 'tensor')
- dense_weight_grad: float32 [2, 1024, 1024], P(None, 'tensor', 'dp')
- dense_bias_grad: float32 [2, 1024], replicated
- fc_in_weight_grad: float32 [2, 1024, 4096], P(None, 'dp', 'tensor')
- fc_in_bias_grad: float32 [2, 4096], P(None, 'tensor')
- fc_out_weight_grad: float32 [2, 4096, 1024], P(None, 'tensor', 'dp')
- fc_out_bias_grad: float32 [2, 1024], replicated
- norm_gain_grad: float32 [2, 2, 1024], replicated
- norm_bias_grad: float32 [2, 2, 1024], replicated
The draws below stay inside these ranges and needn't reach their ends.
Inputs may be any that keep to these rules, and one draw needn't show every extreme that they name: Each row of lengths holds 3 positive lengths that sum to 1024; the largest of each row is exactly 960.
All inputs are finite; a program needn't handle non-finite values.
Results may differ from the reference program's by a relative error of at most 0.023.
Values may be sent and summed in bfloat16 or wider, within the bound.
A program may use at most 192 MiB of HBM per device.

```python
import math
import jax
import jax.numpy as jnp
import numpy as np
from jax import lax

D = 1024
HEADS = 16
HEAD_DIM = 64
ROT = 16
FF = 4096
LAYERS = 2
SEGS = 3
GROUP = 1024
LONGEST = 960
GROUPS = 16
TOKENS = 16384


def level_of(own_key, shape, cuts, least, largest):
    loudness = 1.0
    for dim, shards_of in cuts:
        draws = jax.random.uniform(jax.random.fold_in(jax.random.fold_in(own_key, 6), dim), (shards_of,), jnp.float32, least / len(cuts), largest / len(cuts))
        loudness = loudness * jnp.repeat(jnp.exp(draws), shape[dim] // shards_of).reshape((-1,) + (1,) * (len(shape) - 1 - dim))
    return loudness


def split_up(count, total, bound, lean):
    weights = [(1 << 20) // math.isqrt(grade ** lean) + 1 for grade in range(2, count + 1)]
    surplus, holding = total - bound - (count - 1), [1] * (count - 1)
    while surplus > 0:
        candidates = [i for i in range(count - 1) if holding[i] < bound]
        whole, budget = sum([weights[i] for i in candidates]), surplus
        for i in candidates:
            addition = min(bound - holding[i], max(1, budget * weights[i] // whole), surplus)
            holding[i] = holding[i] + addition
            surplus = surplus - addition
    return np.array([bound] + holding)


def uneven_parts(own_key, number_of, total, reach, slope):
    if number_of == 2:
        one = jax.random.randint(own_key, (), max(1, total - reach), min(reach, total - 1) + 1)
        return jnp.stack([one, total - one])
    tallies = jnp.asarray(split_up(number_of, total, reach, slope), jnp.int32)
    twos = (number_of - 1) // 2
    source_of, taker = tallies[1:1 + 2 * twos:2], tallies[2:2 + 2 * twos:2]
    margin = jnp.minimum(source_of - 1, reach - taker)
    shifted = jax.random.randint(jax.random.fold_in(own_key, 1), (twos,), 0, 1 << 20) % (margin + 1)
    tallies = tallies.at[1:1 + 2 * twos:2].set(source_of - shifted).at[2:2 + 2 * twos:2].set(taker + shifted)
    return tallies[jax.random.permutation(jax.random.fold_in(own_key, 2), number_of)]


def centred(stream_key, dims, deviation, reach, pieces=(), kind=jnp.bfloat16):
    drawn = deviation * jax.random.normal(stream_key, dims, jnp.float32)
    if pieces:
        drawn = drawn * level_of(stream_key, dims, pieces, -0.22, 0.18)
    return jnp.clip(drawn, -reach, reach).astype(kind)


def setup_inputs(seed: int = 0) -> dict:
    seeds = jax.random.split(jax.random.key(seed), 14)
    return {
        "tokens": centred(seeds[0], (TOKENS, D), 1.0, 6.0, ((0, 128),)),
        "lengths": jax.vmap(lambda own: uneven_parts(own, SEGS, GROUP, LONGEST, 2))(jax.random.split(seeds[1], GROUPS)).reshape((GROUPS, SEGS)).astype(jnp.int32),
        "qkv_weight": centred(seeds[2], (LAYERS, D, 3, D), D ** -0.5, 0.1875, ((1, 16), (3, 8))),
        "qkv_bias": centred(seeds[3], (LAYERS, 3, D), 0.5, 3.0, ((2, 8),)),
        "dense_weight": centred(seeds[4], (LAYERS, D, D), (D // 16) ** -0.5, 0.75, ((1, 8), (2, 16))),
        "dense_bias": centred(seeds[5], (LAYERS, D), 0.3, 2.0),
        "fc_in_weight": centred(seeds[6], (LAYERS, D, FF), D ** -0.5, 0.1875, ((1, 16), (2, 8))),
        "fc_in_bias": centred(seeds[7], (LAYERS, FF), 0.5, 3.0, ((1, 8),)),
        "fc_out_weight": centred(seeds[8], (LAYERS, FF, D), FF ** -0.5, 0.09375, ((1, 8), (2, 16))),
        "fc_out_bias": centred(seeds[9], (LAYERS, D), 0.3, 2.0),
        "norm_gain": jnp.clip(1.0 + 0.1 * jax.random.normal(seeds[10], (LAYERS, 2, D), jnp.float32), 0.5, 1.5).astype(jnp.bfloat16),
        "norm_bias": centred(seeds[11], (LAYERS, 2, D), 0.3, 2.0),
        "cotangent": centred(seeds[12], (TOKENS, D), 1.0, 6.0, ((0, 128),)),
    }


HIGHEST = lax.Precision.HIGHEST
EPSILON = 1e-05
MASKED = -1000000000.0

@jax.custom_vjp
def low(v):
    return lax.optimization_barrier(v.astype(jnp.bfloat16)).astype(jnp.float32)

@jax.custom_vjp
def low_back(v):
    return v

def low_keep(v):
    return (low(v), None)

def low_pass(kept, grad):
    return (grad,)

def back_keep(v):
    return (v, None)

def back_low(kept, grad):
    return (low(grad),)
low.defvjp(low_keep, low_pass)
low_back.defvjp(back_keep, back_low)

def layer_norm(stream, scale_gain, shift_bias):
    average = lax.optimization_barrier(jnp.mean(stream, axis=-1, keepdims=True))
    centered = stream - average
    spread = lax.optimization_barrier(jnp.mean(centered * centered, axis=-1, keepdims=True))
    return centered * lax.rsqrt(spread + EPSILON) * scale_gain + shift_bias

def rotate(vectors, cosine, sine_table):
    half_rot = cosine.shape[-1]
    first_rot = vectors[..., :half_rot]
    second = vectors[..., half_rot:2 * half_rot]
    untouched = vectors[..., 2 * half_rot:]
    return jnp.concatenate([first_rot * cosine - second * sine_table, second * cosine + first_rot * sine_table, untouched], axis=-1)

def positions(lengths, group_rows):
    endings = jnp.cumsum(lengths).astype(jnp.int32)
    starts = (endings - lengths).astype(jnp.int32)
    row_ids = jnp.arange(group_rows, dtype=jnp.int32)
    member = (row_ids[:, None] >= starts[None, :]) & (row_ids[:, None] < endings[None, :])
    numbers = jnp.arange(lengths.shape[0], dtype=jnp.int32)
    segment = lax.optimization_barrier(jnp.sum(jnp.where(member, numbers[None, :], 0), axis=1)).astype(jnp.int32)
    opening = lax.optimization_barrier(jnp.sum(jnp.where(member, starts[None, :], 0), axis=1)).astype(jnp.int32)
    return (segment, (row_ids - opening).astype(jnp.int32))

def group_forward(stream, params, segment, cosine, sine_table):
    qkv_w, qkv_b, dense_w, dense_b, in_w, in_b, out_w, out_b, gains, shifts = params
    group_rows = stream.shape[0]
    row_ids = jnp.arange(group_rows, dtype=jnp.int32)
    allowed = (segment[:, None] == segment[None, :]) & (row_ids[None, :] <= row_ids[:, None])
    score_scale = HEAD_DIM ** (-0.5)
    head_shape = (group_rows, HEADS, HEAD_DIM)
    for layer_index in range(LAYERS):
        normed_attn = low(layer_norm(stream, gains[layer_index, 0], shifts[layer_index, 0]))
        normed_mlp = low(layer_norm(stream, gains[layer_index, 1], shifts[layer_index, 1]))
        mixed_proj = jnp.einsum('gd,dcf->gcf', normed_attn, qkv_w[layer_index], precision=HIGHEST) + qkv_b[layer_index]
        queries = low(rotate(low_back(mixed_proj[:, 0]).reshape(head_shape), cosine, sine_table))
        keys_rot = low(rotate(low_back(mixed_proj[:, 1]).reshape(head_shape), cosine, sine_table))
        values_in = low(low_back(mixed_proj[:, 2]).reshape(head_shape))
        scores = low_back(jnp.einsum('qhe,khe->hqk', queries, keys_rot, precision=HIGHEST) * score_scale)
        scores = jnp.where(allowed[None], scores, MASKED)
        probability = low(jax.nn.softmax(scores, axis=-1))
        attended = jnp.einsum('hqk,khe->qhe', probability, values_in, precision=HIGHEST).reshape(group_rows, D)
        attended = low(low_back(attended))
        pre_gelu = jnp.dot(normed_mlp, in_w[layer_index], precision=HIGHEST) + in_b[layer_index]
        hidden = low(jax.nn.gelu(low_back(pre_gelu), approximate=False))
        branch = low_back(jnp.dot(attended, dense_w[layer_index], precision=HIGHEST) + jnp.dot(hidden, out_w[layer_index], precision=HIGHEST))
        stream = stream + branch + dense_b[layer_index] + out_b[layer_index]
    return stream

def add_pair(earlier, later):
    return earlier + later

def reference(tokens, lengths, qkv_weight, qkv_bias, dense_weight, dense_bias, fc_in_weight, fc_in_bias, fc_out_weight, fc_out_bias, norm_gain, norm_bias, cotangent):
    params = tuple((array.astype(jnp.float32) for array in (qkv_weight, qkv_bias, dense_weight, dense_bias, fc_in_weight, fc_in_bias, fc_out_weight, fc_out_bias, norm_gain, norm_bias)))
    streams = tokens.astype(jnp.float32).reshape(GROUPS, GROUP, D)
    grads_in = cotangent.astype(jnp.float32).reshape(GROUPS, GROUP, D)
    half_rot = ROT // 2
    frequency = 10000.0 ** (-(2.0 * jnp.arange(half_rot, dtype=jnp.float32)) / ROT)

    def one_group(totals, item):
        group_stream, group_grad, group_lengths = item
        segment, position = positions(group_lengths, GROUP)
        angles = position.astype(jnp.float32)[:, None] * frequency[None, :]
        cosine = jnp.cos(angles)[:, None, :]
        sine_table = jnp.sin(angles)[:, None, :]

        def forward_fn(stream_in, param_in):
            return group_forward(stream_in, param_in, segment, cosine, sine_table)
        result, backward_fn = jax.vjp(forward_fn, group_stream, params)
        stream_grad, param_grads = backward_fn(group_grad)
        totals = jax.tree.map(add_pair, totals, param_grads)
        return (totals, (result.astype(jnp.bfloat16), stream_grad))
    zero_grads = jax.tree.map(jnp.zeros_like, params)
    totals, (results, stream_grads) = lax.scan(one_group, zero_grads, (streams, grads_in, lengths))
    return (results.reshape(TOKENS, D), stream_grads.reshape(TOKENS, D), totals[0], totals[1], totals[2], totals[3], totals[4], totals[5], totals[6], totals[7], totals[8], totals[9])
```

```python
from functools import partial

import jax
import jax.numpy as jnp
from jax import lax
from jax.experimental import pallas as pl
from jax.experimental.pallas import tpu as pltpu
from jax.sharding import PartitionSpec as P

MESH = pl.DeviceIdType.MESH
HEAD_DIM = 64
ROT = 16
EPSILON = 1e-05
MASKED = -1000000000.0
BF = jnp.bfloat16
F32 = jnp.float32
ANY = pl.BlockSpec(memory_space=pl.ANY)
VM = pl.BlockSpec(memory_space=pltpu.VMEM)

T_DELTAS = [(y, h) for y in (1, 3, 2, 0) for h in (0, 1) if y or h]
C_DELTAS = [(a, z) for z in (1, 3, 2, 0) for a in (0, 1) if a or z]


def coords():
    d = lax.axis_index("dp")
    t = lax.axis_index("tensor")
    return d // 8, lax.rem(d // 2, 4), lax.rem(d, 2), t // 2, lax.rem(t, 2)


def t_peer(y, h, delta):
    return lax.rem(y + delta[0], 4) * 2 + lax.rem(h + delta[1], 2)


def c_peer(a, z, delta):
    return lax.rem(a + delta[0], 2) * 4 + lax.rem(z + delta[1], 4)


def greet(d, t, tensor_peers, dp_peers):
    barrier = pltpu.get_barrier_semaphore()
    for p in tensor_peers:
        pl.semaphore_signal(barrier, inc=1, device_id=(d, p), device_id_type=MESH)
    for p in dp_peers:
        pl.semaphore_signal(barrier, inc=1, device_id=(p, t), device_id_type=MESH)
    pl.semaphore_wait(barrier, len(tensor_peers) + len(dp_peers))


def send(src, dst, ssem, rsem, device):
    copy = pltpu.make_async_remote_copy(
        src_ref=src, dst_ref=dst, send_sem=ssem, recv_sem=rsem, device_id=device, device_id_type=MESH
    )
    copy.start()
    return copy


def tensor_gather_start(src, dst, d, t, tp, ssem, rsem):
    rows = src.shape[0]
    place = dst.at[pl.ds(pl.multiple_of(t * rows, rows), rows)]
    return [send(src, place, ssem.at[i], rsem.at[i], (d, p)) for i, p in enumerate(tp)]


def tensor_scatter_start(src, buf, d, tp, ssem, rsem):
    rows = buf.shape[1]
    return [
        send(src.at[pl.ds(pl.multiple_of(p * rows, rows), rows)], buf.at[i], ssem.at[i], rsem.at[i], (d, p))
        for i, p in enumerate(tp)
    ]


def dp_gather_start(src, dst, chip, core, t, cp, ssem, rsem):
    rows = src.shape[0]
    place = dst.at[pl.ds(pl.multiple_of((chip * 2 + core) * rows, rows), rows)]
    first = [send(src, place, ssem.at[i], rsem.at[i], (p * 2 + core, t)) for i, p in enumerate(cp)]
    mine = send(src, place, ssem.at[7], rsem.at[7], (chip * 2 + 1 - core, t))
    return first, mine


def dp_gather_finish(first, mine, dst, rows, chip, core, t, sources, ssem, rsem):
    second = []
    for i, s in enumerate(sources):
        first[i].wait_recv()
        place = dst.at[pl.ds(pl.multiple_of((s * 2 + core) * rows, rows), rows)]
        second.append(send(place, place, ssem.at[8 + i], rsem.at[8 + i], (chip * 2 + 1 - core, t)))
    for c in first:
        c.wait_send()
    mine.wait()
    for c in second:
        c.wait()


def peers():
    a, z, core, y, h = coords()
    d = lax.axis_index("dp")
    t = lax.axis_index("tensor")
    chip = a * 4 + z
    tp = [t_peer(y, h, x) for x in T_DELTAS]
    cp = [c_peer(a, z, x) for x in C_DELTAS]
    back = [c_peer(a, z, (x[0], (4 - x[1]) % 4)) for x in C_DELTAS]
    return d, t, chip, core, tp, cp, back


def open_kernel(x_ref, w_ref, xg_ref, wg_ref, ts, tr, ds_, dr, ls):
    d, t, chip, core, tp, cp, back = peers()
    rows = x_ref.shape[0]
    wrows = w_ref.shape[0]
    own = pltpu.make_async_copy(x_ref, xg_ref.at[pl.ds(pl.multiple_of(t * rows, rows), rows)], ls.at[0])
    own.start()
    own_w = pltpu.make_async_copy(w_ref, wg_ref.at[pl.ds(pl.multiple_of(d * wrows, wrows), wrows)], ls.at[1])
    own_w.start()
    greet(d, t, tp, [p * 2 + core for p in cp] + [chip * 2 + 1 - core])
    xs = tensor_gather_start(x_ref, xg_ref, d, t, tp, ts, tr)
    first, mine = dp_gather_start(w_ref, wg_ref, chip, core, t, cp, ds_, dr)
    dp_gather_finish(first, mine, wg_ref, wrows, chip, core, t, back, ds_, dr)
    for c in xs:
        c.wait()
    own.wait()
    own_w.wait()


def open_call(x, w, cid):
    return pl.pallas_call(
        open_kernel,
        out_shape=(
            jax.ShapeDtypeStruct((x.shape[0] * 8, x.shape[1]), x.dtype),
            jax.ShapeDtypeStruct((w.shape[0] * 16, w.shape[1]), w.dtype),
        ),
        in_specs=[ANY, ANY],
        out_specs=(ANY, ANY),
        scratch_shapes=[
            pltpu.SemaphoreType.DMA((7,)),
            pltpu.SemaphoreType.DMA((7,)),
            pltpu.SemaphoreType.DMA((15,)),
            pltpu.SemaphoreType.DMA((15,)),
            pltpu.SemaphoreType.DMA((2,)),
        ],
        compiler_params=pltpu.CompilerParams(collective_id=cid, has_side_effects=True),
        cost_estimate=pl.CostEstimate(flops=0, bytes_accessed=80_000_000, transcendentals=0),
        name="gather_weights_and_rows",
    )(x, w)


def summed(own, buf):
    total = own.astype(F32)
    for i in range(7):
        total = total + buf[i].astype(F32)
    return total


def normed(x):
    average = jnp.mean(x, axis=-1, keepdims=True)
    centered = x - average
    inv = lax.rsqrt(jnp.mean(centered * centered, axis=-1, keepdims=True) + EPSILON)
    return centered * inv, inv


def middle_kernel(
    part_ref, stream_ref, bias_ref, w_ref, stream_out, xg_ref, wg_ref,
    own_v, buf, xhat_v, rs_s, rs_r, ts, tr, ds_, dr, ls,
):
    d, t, chip, core, tp, cp, back = peers()
    rows = stream_ref.shape[0]
    wrows = w_ref.shape[0]
    own = pltpu.make_async_copy(part_ref.at[pl.ds(pl.multiple_of(t * rows, rows), rows)], own_v, ls.at[0])
    own.start()
    own_w = pltpu.make_async_copy(w_ref, wg_ref.at[pl.ds(pl.multiple_of(d * wrows, wrows), wrows)], ls.at[1])
    own_w.start()
    greet(d, t, tp, [p * 2 + core for p in cp] + [chip * 2 + 1 - core])
    rs = tensor_scatter_start(part_ref, buf, d, tp, rs_s, rs_r)
    first, mine = dp_gather_start(w_ref, wg_ref, chip, core, t, cp, ds_, dr)
    own.wait()
    for c in rs:
        c.wait()
    stream = stream_ref[...] + summed(own_v[...], buf) + bias_ref[...]
    stream_out[...] = stream
    xhat_v[...] = normed(stream)[0].astype(BF)
    own2 = pltpu.make_async_copy(xhat_v, xg_ref.at[pl.ds(pl.multiple_of(t * rows, rows), rows)], ls.at[0])
    own2.start()
    xs = tensor_gather_start(xhat_v, xg_ref, d, t, tp, ts, tr)
    dp_gather_finish(first, mine, wg_ref, wrows, chip, core, t, back, ds_, dr)
    for c in xs:
        c.wait()
    own2.wait()
    own_w.wait()


def middle_call(part, stream, bias, w, cid):
    rows, width = stream.shape
    dma = pltpu.SemaphoreType.DMA
    return pl.pallas_call(
        middle_kernel,
        out_shape=(
            jax.ShapeDtypeStruct(stream.shape, F32),
            jax.ShapeDtypeStruct(part.shape, BF),
            jax.ShapeDtypeStruct((w.shape[0] * 16, w.shape[1]), w.dtype),
        ),
        in_specs=[ANY, VM, VM, ANY],
        out_specs=(VM, ANY, ANY),
        scratch_shapes=[
            pltpu.VMEM((rows, width), BF),
            pltpu.VMEM((7, rows, width), BF),
            pltpu.VMEM((rows, width), BF),
            dma((7,)), dma((7,)), dma((7,)), dma((7,)), dma((15,)), dma((15,)), dma((2,)),
        ],
        compiler_params=pltpu.CompilerParams(
            collective_id=cid, has_side_effects=True, vmem_limit_bytes=32 * 2**20
        ),
        cost_estimate=pl.CostEstimate(flops=0, bytes_accessed=150_000_000, transcendentals=0),
        name="sum_rows_and_gather",
    )(part, stream, bias, w)


def dp_scatter_core(dw_ref, mine_v, core_buf, chip, core, t, ssem, rsem, lsem):
    mine = pltpu.make_async_copy(dw_ref.at[:, core], mine_v, lsem)
    mine.start()
    swap = send(dw_ref.at[:, 1 - core], core_buf, ssem, rsem, (chip * 2 + 1 - core, t))
    return mine, swap


def dp_scatter_chips(mine, swap, mine_v, core_buf, chip_buf, core, t, cp, ssem, rsem):
    mine.wait()
    swap.wait()
    copies = []
    for i, p in enumerate(cp):
        mine_v[p] = (mine_v[p].astype(F32) + core_buf[p].astype(F32)).astype(BF)
        copies.append(send(mine_v.at[p], chip_buf.at[i], ssem.at[i], rsem.at[i], (p * 2 + core, t)))
    return copies


def dp_scatter_finish(copies, mine_v, core_buf, chip_buf, chip, out_ref):
    for c in copies:
        c.wait()
    total = mine_v[chip].astype(F32) + core_buf[chip].astype(F32)
    for i in range(7):
        total = total + chip_buf[i].astype(F32)
    out_ref[...] = total


def stream_back(total, grad, stream):
    xhat, inv = normed(stream)
    first = jnp.mean(total, axis=-1, keepdims=True)
    second = jnp.mean(total * xhat, axis=-1, keepdims=True)
    return grad + inv * (total - first - xhat * second)


def turn_kernel(
    part_ref, grad_ref, stream_ref, dw_ref, grad_out, gg_ref, dw_out,
    own_v, buf, low_v, mine_v, core_buf, chip_buf, rs_s, rs_r, ts, tr, ds_, dr, ls,
):
    d, t, chip, core, tp, cp, back = peers()
    rows = stream_ref.shape[0]
    own = pltpu.make_async_copy(part_ref.at[pl.ds(pl.multiple_of(t * rows, rows), rows)], own_v, ls.at[0])
    own.start()
    greet(d, t, tp, [p * 2 + core for p in cp] + [chip * 2 + 1 - core])
    mine, swap = dp_scatter_core(dw_ref, mine_v, core_buf, chip, core, t, ds_.at[7], dr.at[7], ls.at[1])
    rs = tensor_scatter_start(part_ref, buf, d, tp, rs_s, rs_r)
    copies = dp_scatter_chips(mine, swap, mine_v, core_buf, chip_buf, core, t, cp, ds_, dr)
    own.wait()
    for c in rs:
        c.wait()
    grad = stream_back(summed(own_v[...], buf), grad_ref[...], stream_ref[...])
    grad_out[...] = grad
    low_v[...] = grad.astype(BF)
    own2 = pltpu.make_async_copy(low_v, gg_ref.at[pl.ds(pl.multiple_of(t * rows, rows), rows)], ls.at[0])
    own2.start()
    xs = tensor_gather_start(low_v, gg_ref, d, t, tp, ts, tr)
    dp_scatter_finish(copies, mine_v, core_buf, chip_buf, chip, dw_out)
    for c in xs:
        c.wait()
    own2.wait()


def turn_call(part, grad, stream, dw, cid):
    rows, width = stream.shape
    wrows, wcols = dw.shape[0] // 16, dw.shape[1]
    dma = pltpu.SemaphoreType.DMA
    return pl.pallas_call(
        turn_kernel,
        out_shape=(
            jax.ShapeDtypeStruct(stream.shape, F32),
            jax.ShapeDtypeStruct(part.shape, BF),
            jax.ShapeDtypeStruct((wrows, wcols), F32),
        ),
        in_specs=[ANY, VM, VM, ANY],
        out_specs=(VM, ANY, VM),
        scratch_shapes=[
            pltpu.VMEM((rows, width), BF),
            pltpu.VMEM((7, rows, width), BF),
            pltpu.VMEM((rows, width), BF),
            pltpu.VMEM((8, wrows, wcols), BF),
            pltpu.VMEM((8, wrows, wcols), BF),
            pltpu.VMEM((7, wrows, wcols), BF),
            dma((7,)), dma((7,)), dma((7,)), dma((7,)), dma((8,)), dma((8,)), dma((2,)),
        ],
        compiler_params=pltpu.CompilerParams(
            collective_id=cid, has_side_effects=True, vmem_limit_bytes=32 * 2**20
        ),
        cost_estimate=pl.CostEstimate(flops=0, bytes_accessed=150_000_000, transcendentals=0),
        name="sum_gradients_and_gather",
    )(part, grad, stream, dw.reshape(8, 2, wrows, wcols))


def last_kernel(
    part_ref, grad_ref, stream_ref, dw_ref, small_ref, cols_ref, grad_out, dw_out, small_out, cols_out,
    own_v, buf, mine_v, core_buf, chip_buf, small_buf, both_v, both_buf, sum_v,
    rs_s, rs_r, ds_, dr, ls, ss, sr, bs, br, gs, gr,
):
    d, t, chip, core, tp, cp, back = peers()
    rows = stream_ref.shape[0]
    own = pltpu.make_async_copy(part_ref.at[pl.ds(pl.multiple_of(t * rows, rows), rows)], own_v, ls.at[0])
    own.start()
    others = [p * 2 + core for p in cp] + [p * 2 + 1 - core for p in cp] + [chip * 2 + 1 - core]
    greet(d, t, tp, others)
    mine, swap = dp_scatter_core(dw_ref, mine_v, core_buf, chip, core, t, ds_.at[7], dr.at[7], ls.at[1])
    small = [
        send(small_ref.at[p], small_buf.at[i], ss.at[i], sr.at[i], (d, p)) for i, p in enumerate(tp)
    ]
    rs = tensor_scatter_start(part_ref, buf, d, tp, rs_s, rs_r)
    copies = dp_scatter_chips(mine, swap, mine_v, core_buf, chip_buf, core, t, cp, ds_, dr)
    for c in small:
        c.wait()
    total = small_ref[t]
    for i in range(7):
        total = total + small_buf[i]
    both_v[0:16] = total
    both_v[16:32] = cols_ref[...]
    both = [send(both_v, both_buf.at[i], bs.at[i], br.at[i], (p, t)) for i, p in enumerate(others)]
    for c in both:
        c.wait()
    total = both_v[...]
    for i in range(15):
        total = total + both_buf[i]
    cols_out[...] = total[16:32]
    sum_v[...] = total[0:16]
    small_out[t] = total[0:16]
    spread = [send(sum_v, small_out.at[t], gs.at[i], gr.at[i], (d, p)) for i, p in enumerate(tp)]
    own.wait()
    for c in rs:
        c.wait()
    grad_out[...] = stream_back(summed(own_v[...], buf), grad_ref[...], stream_ref[...])
    dp_scatter_finish(copies, mine_v, core_buf, chip_buf, chip, dw_out)
    for c in spread:
        c.wait()


def last_call(part, grad, stream, dw, small, cols, cid):
    rows, width = stream.shape
    wrows, wcols = dw.shape[0] // 16, dw.shape[1]
    dma = pltpu.SemaphoreType.DMA
    return pl.pallas_call(
        last_kernel,
        out_shape=(
            jax.ShapeDtypeStruct(stream.shape, F32),
            jax.ShapeDtypeStruct((wrows, wcols), F32),
            jax.ShapeDtypeStruct((8, 16, 128), F32),
            jax.ShapeDtypeStruct((16, 128), F32),
        ),
        in_specs=[ANY, VM, VM, ANY, VM, VM],
        out_specs=(VM, VM, VM, VM),
        scratch_shapes=[
            pltpu.VMEM((rows, width), BF),
            pltpu.VMEM((7, rows, width), BF),
            pltpu.VMEM((8, wrows, wcols), BF),
            pltpu.VMEM((8, wrows, wcols), BF),
            pltpu.VMEM((7, wrows, wcols), BF),
            pltpu.VMEM((7, 16, 128), F32),
            pltpu.VMEM((32, 128), F32),
            pltpu.VMEM((15, 32, 128), F32),
            pltpu.VMEM((16, 128), F32),
            dma((7,)), dma((7,)), dma((8,)), dma((8,)), dma((2,)),
            dma((7,)), dma((7,)), dma((15,)), dma((15,)), dma((7,)), dma((7,)),
        ],
        compiler_params=pltpu.CompilerParams(
            collective_id=cid, has_side_effects=True, vmem_limit_bytes=32 * 2**20
        ),
        cost_estimate=pl.CostEstimate(flops=0, bytes_accessed=100_000_000, transcendentals=0),
        name="sum_all_gradients",
    )(part, grad, stream, dw.reshape(8, 2, wrows, wcols), small, cols)


def rotate(vectors, cosine, sine_table):
    half_rot = cosine.shape[-1]
    first_rot = vectors[..., :half_rot]
    second = vectors[..., half_rot : 2 * half_rot]
    untouched = vectors[..., 2 * half_rot :]
    return jnp.concatenate(
        [
            first_rot * cosine - second * sine_table,
            second * cosine + first_rot * sine_table,
            untouched,
        ],
        axis=-1,
    )


def positions(lengths, group_rows):
    endings = jnp.cumsum(lengths)
    starts = endings - lengths
    row_ids = jnp.arange(group_rows, dtype=jnp.int32)
    member = (row_ids[:, None] >= starts[None, :]) & (row_ids[:, None] < endings[None, :])
    numbers = jnp.arange(lengths.shape[0], dtype=jnp.int32)
    segment = jnp.sum(jnp.where(member, numbers[None, :], 0), axis=1)
    opening = jnp.sum(jnp.where(member, starts[None, :], 0), axis=1)
    return (segment, row_ids - opening)


def visible(segment, block_start, block_rows):
    group_rows = segment.shape[0]
    query_ids = block_start + jnp.arange(block_rows, dtype=jnp.int32)
    key_ids = jnp.arange(group_rows, dtype=jnp.int32)
    same_doc = segment[block_start : block_start + block_rows][:, None] == segment[None, :]
    return same_doc & (key_ids[None, :] <= query_ids[:, None])


def block_scores(block_queries, keys_rot, segment, block_start, block_rows, score_scale):
    scores = (
        jnp.einsum("bhe,khe->hbk", block_queries, keys_rot, preferred_element_type=F32)
        * score_scale
    )
    return jnp.where(visible(segment, block_start, block_rows)[None], scores, MASKED)


def attend(queries, keys_rot, values_in, segment, block_rows, score_scale):
    outputs = []
    log_totals = []
    for block_start in range(0, queries.shape[0], block_rows):
        block_queries = queries[block_start : block_start + block_rows]
        scores = block_scores(
            block_queries, keys_rot, segment, block_start, block_rows, score_scale
        )
        row_max = jnp.max(scores, axis=-1, keepdims=True)
        exponent = jnp.exp(scores - row_max)
        row_total = jnp.sum(exponent, axis=-1, keepdims=True)
        probability = (exponent / row_total).astype(BF)
        outputs.append(
            jnp.einsum("hbk,khe->bhe", probability, values_in, preferred_element_type=F32)
        )
        log_totals.append(row_max + jnp.log(row_total))
    return (jnp.concatenate(outputs, axis=0), log_totals)


def attend_back(
    queries, keys_rot, values_in, log_totals, attended_grad, segment, block_rows, score_scale
):
    keys_grad = jnp.zeros(keys_rot.shape, F32)
    values_grad = jnp.zeros(values_in.shape, F32)
    query_parts = []
    for block_index, block_start in enumerate(range(0, queries.shape[0], block_rows)):
        block_queries = queries[block_start : block_start + block_rows]
        block_grad = attended_grad[block_start : block_start + block_rows]
        scores = block_scores(
            block_queries, keys_rot, segment, block_start, block_rows, score_scale
        )
        probability = jnp.exp(scores - log_totals[block_index])
        prob_grad = jnp.einsum("bhe,khe->hbk", block_grad, values_in, preferred_element_type=F32)
        centre = jnp.sum(probability * prob_grad, axis=-1, keepdims=True)
        score_grad = (probability * (prob_grad - centre)).astype(BF)
        query_parts.append(
            jnp.einsum("hbk,khe->bhe", score_grad, keys_rot, preferred_element_type=F32)
            * score_scale
        )
        keys_grad = (
            keys_grad
            + jnp.einsum("hbk,bhe->khe", score_grad, block_queries, preferred_element_type=F32)
            * score_scale
        )
        values_grad = values_grad + jnp.einsum(
            "hbk,bhe->khe", probability.astype(BF), block_grad, preferred_element_type=F32
        )
    return (jnp.concatenate(query_parts, axis=0), keys_grad, values_grad)


def nn(a, b):
    return jnp.dot(a, b, preferred_element_type=F32)


def tn(a, b):
    return lax.dot_general(a, b, (((0,), (0,)), ((), ())), preferred_element_type=F32)


def nt(a, b):
    return lax.dot_general(a, b, (((1,), (1,)), ((), ())), preferred_element_type=F32)


def forward(xhat, w, gain, shift, qkv_b, in_b, segment, cosine, sine, block_rows):
    x32 = xhat.astype(F32)
    n1 = (x32 * gain[0] + shift[0]).astype(BF)
    n2 = (x32 * gain[1] + shift[1]).astype(BF)
    proj = nn(n1, w[:, 0:384]) + qkv_b
    rows = xhat.shape[0]
    shape = (rows, 2, HEAD_DIM)
    q = rotate(proj[:, 0:128].reshape(shape), cosine, sine).astype(BF)
    k = rotate(proj[:, 128:256].reshape(shape), cosine, sine).astype(BF)
    v = proj[:, 256:384].reshape(shape).astype(BF)
    attended, logs = attend(q, k, v, segment, block_rows, HEAD_DIM**-0.5)
    attended = attended.reshape(rows, 128).astype(BF)
    pre = nn(n2, w[:, 384:896]) + in_b
    hidden = jax.nn.gelu(pre, approximate=False).astype(BF)
    cat = jnp.concatenate([attended, hidden], axis=1)
    branch = nt(cat, w[:, 896:1536]).astype(BF)
    return branch, (n1, n2, q, k, v, logs, pre, cat)


def backward(grad, xhat, w, gain, kept, segment, cosine, sine, block_rows):
    n1, n2, q, k, v, logs, pre, cat = kept
    rows = xhat.shape[0]
    d_out = tn(grad, cat).astype(BF)
    cat_grad = nn(grad, w[:, 896:1536])
    att_grad = cat_grad[:, 0:128].astype(BF).reshape(q.shape)
    gelu_back = jax.vjp(partial(jax.nn.gelu, approximate=False), pre)[1]
    pre_grad = gelu_back(cat_grad[:, 128:640])[0].astype(BF)
    qg, kg, vg = attend_back(q, k, v, logs, att_grad, segment, block_rows, HEAD_DIM**-0.5)
    proj_grad = jnp.concatenate(
        [
            rotate(qg, cosine, -sine).reshape(rows, 128),
            rotate(kg, cosine, -sine).reshape(rows, 128),
            vg.reshape(rows, 128),
        ],
        axis=1,
    ).astype(BF)
    dw = jnp.concatenate([tn(n1, proj_grad).astype(BF), tn(n2, pre_grad).astype(BF), d_out], axis=1)
    cols = jnp.concatenate(
        [jnp.sum(proj_grad.astype(F32), axis=0), jnp.sum(pre_grad.astype(F32), axis=0)]
    )
    n1_grad = nt(proj_grad, w[:, 0:384])
    n2_grad = nt(pre_grad, w[:, 384:896])
    x32 = xhat.astype(F32)
    small = jnp.stack(
        [
            jnp.sum(n1_grad * x32, axis=0),
            jnp.sum(n2_grad * x32, axis=0),
            jnp.sum(n1_grad, axis=0),
            jnp.sum(n2_grad, axis=0),
        ]
    )
    part = (n1_grad * gain[0] + n2_grad * gain[1]).astype(BF)
    return part, dw, cols, small


def local(
    tokens,
    lengths,
    qkv_weight,
    qkv_bias,
    dense_weight,
    dense_bias,
    fc_in_weight,
    fc_in_bias,
    fc_out_weight,
    fc_out_bias,
    norm_gain,
    norm_bias,
    cotangent,
):
    rows = tokens.shape[0]
    group_rows = rows * 8
    block_rows = 512
    segment, position = positions(lengths[0], group_rows)
    half_rot = ROT // 2
    frequency = 10000.0 ** (-(2.0 * jnp.arange(half_rot, dtype=F32)) / ROT)
    angles = position.astype(F32)[:, None] * frequency[None, :]
    cosine = jnp.cos(angles)[:, None, :]
    sine = jnp.sin(angles)[:, None, :]
    gain = norm_gain.astype(F32)
    shift = norm_bias.astype(F32)
    qkv_b = qkv_bias.astype(F32).reshape(2, 384)
    in_b = fc_in_bias.astype(F32)
    out_b = dense_bias.astype(F32) + fc_out_bias.astype(F32)
    shards = [
        jnp.concatenate(
            [
                qkv_weight[i].reshape(64, 384),
                fc_in_weight[i],
                dense_weight[i].T,
                fc_out_weight[i].T,
            ],
            axis=1,
        )
        for i in range(2)
    ]
    stream0 = tokens.astype(F32)
    xhat0 = normed(stream0)[0].astype(BF)
    grad2 = cotangent.astype(F32)
    grad2_rows = lax.all_gather(cotangent, "tensor", axis=0, tiled=True)

    xg0, w0 = open_call(xhat0, shards[0], 1)
    part, kept0 = forward(xg0, w0, gain[0], shift[0], qkv_b[0], in_b[0], segment, cosine, sine, block_rows)
    stream1, xg1, w1 = middle_call(part, stream0, out_b[0:1], shards[1], 2)
    part, kept1 = forward(xg1, w1, gain[1], shift[1], qkv_b[1], in_b[1], segment, cosine, sine, block_rows)
    branch = lax.psum_scatter(part, "tensor", scatter_dimension=0, tiled=True)
    output = (stream1 + branch.astype(F32) + out_b[1]).astype(BF)

    part, dw1, cols1, small1 = backward(
        grad2_rows, xg1, w1, gain[1], kept1, segment, cosine, sine, block_rows
    )
    grad1, grad1_rows, dw1 = turn_call(part, grad2, stream1, dw1, 3)
    part, dw0, cols0, small0 = backward(
        grad1_rows, xg0, w0, gain[0], kept0, segment, cosine, sine, block_rows
    )
    small = jnp.concatenate(
        [
            small0,
            small1,
            jnp.sum(grad1, axis=0, keepdims=True),
            jnp.sum(grad2, axis=0, keepdims=True),
            jnp.zeros((6, 1024), F32),
        ]
    )
    small = small.reshape(16, 8, 128).swapaxes(0, 1)
    cols = jnp.concatenate([cols0, cols1, jnp.zeros((256,), F32)]).reshape(16, 128)
    input_grad, dw0, small, cols = last_call(part, grad1, stream0, dw0, small, cols, 4)
    small = small.swapaxes(0, 1).reshape(16, 1024)
    cols = cols.reshape(2048)[:1792].reshape(2, 896)
    dw = jnp.stack([dw0, dw1])
    bias_grad = small[8:10]
    norms = small[0:8].reshape(2, 2, 2, 1024)
    return (
        output,
        input_grad,
        dw[:, :, 0:384].reshape(2, 64, 3, 128),
        cols[:, 0:384].reshape(2, 3, 128),
        dw[:, :, 896:1024].swapaxes(1, 2),
        bias_grad,
        dw[:, :, 384:896],
        cols[:, 384:896],
        dw[:, :, 1024:1536].swapaxes(1, 2),
        bias_grad,
        norms[:, 0],
        norms[:, 1],
    )


def solution(mesh):
    return jax.shard_map(
        local,
        mesh=mesh,
        in_specs=(
            P(("dp", "tensor"), None),
            P("dp", None),
            P(None, "dp", None, "tensor"),
            P(None, None, "tensor"),
            P(None, "tensor", "dp"),
            P(),
            P(None, "dp", "tensor"),
            P(None, "tensor"),
            P(None, "tensor", "dp"),
            P(),
            P(),
            P(),
            P(("dp", "tensor"), None),
        ),
        out_specs=(
            P(("dp", "tensor"), None),
            P(("dp", "tensor"), None),
            P(None, "dp", None, "tensor"),
            P(None, None, "tensor"),
            P(None, "tensor", "dp"),
            P(),
            P(None, "dp", "tensor"),
            P(None, "tensor"),
            P(None, "tensor", "dp"),
            P(),
            P(),
            P(),
        ),
        check_vma=False,
    )
```

```python
import jax
import jax.numpy as jnp
import numpy as np
from jax import lax
from jax.experimental import pallas as pl
from jax.experimental.pallas import tpu as pltpu
from jax.sharding import PartitionSpec as P

MESH = pl.DeviceIdType.MESH
HEAD_DIM = 64
ROT = 16
EPSILON = 1e-05
MASKED = -1000000000.0
ROWS = 256
BF = jnp.bfloat16
F32 = jnp.float32
ANY = pl.BlockSpec(memory_space=pl.ANY)
VM = pl.BlockSpec(memory_space=pltpu.VMEM)


class Net:
    def __init__(self, ring, pair, index, device):
        self.ring, self.pair, self.index_of, self.device_of = ring, pair, index, device

    def block(self, r, p):
        return self.index_of(lax.rem(self.ring + r, 4), lax.rem(self.pair + p, 2))

    def device(self, r, p):
        return self.device_of(self.block(r, p))


def place():
    d = lax.axis_index("dp")
    t = lax.axis_index("tensor")
    core = lax.rem(d, 2)
    tensor = Net(t // 2, lax.rem(t, 2), lambda r, p: r * 2 + p, lambda i: (d, i))
    chips = Net(lax.rem(d // 2, 4), d // 8, lambda r, p: p * 4 + r, lambda i: (i * 2 + core, t))
    return d, t, core, tensor, chips


PEERS = [(1, 0), (3, 0), (2, 0), (0, 1)]


def greet(devices):
    barrier = pltpu.get_barrier_semaphore()
    for device in devices:
        pl.semaphore_signal(barrier, inc=1, device_id=device, device_id_type=MESH)
    pl.semaphore_wait(barrier, len(devices))


def send(src, dst, sems, i, device):
    copy = pltpu.make_async_remote_copy(
        src_ref=src,
        dst_ref=dst,
        send_sem=sems.at[0, i],
        recv_sem=sems.at[1, i],
        device_id=device,
        device_id_type=MESH,
    )
    copy.start()
    return copy


class Gather:
    def __init__(self, net, dst, rows, sems, place_of=None):
        self.net, self.dst, self.rows, self.sems = net, dst, rows, sems
        self.place_of = place_of or (lambda i: i)

    def at(self, r, p):
        i = self.place_of(self.net.block(r, p))
        return self.dst.at[pl.ds(pl.multiple_of(i * self.rows, self.rows), self.rows)]

    def start(self, src):
        net, sems = self.net, self.sems
        mine = self.at(0, 0)
        self.across = send(src, mine, sems, 0, net.device(0, 1))
        self.opposite = send(src, mine, sems, 1, net.device(2, 0))
        self.up = send(src, mine, sems, 2, net.device(1, 0))
        self.down = send(src, mine, sems, 3, net.device(3, 0))

    def middle(self, seen=lambda block: None):
        net, sems = self.net, self.sems
        self.across.wait_recv()
        block = self.at(0, 1)
        self.up2 = send(block, block, sems, 4, net.device(1, 0))
        self.down2 = send(block, block, sems, 5, net.device(3, 0))
        seen(block)
        self.opposite.wait_recv()
        block = self.at(2, 0)
        self.across2 = send(block, block, sems, 6, net.device(0, 1))
        seen(block)

    def finish(self, seen=lambda block: None):
        for copy, r, p in (
            (self.up, 3, 0), (self.down, 1, 0), (self.up2, 3, 1), (self.down2, 1, 1), (self.across2, 2, 1)
        ):
            copy.wait_recv()
            seen(self.at(r, p))
        for copy in (
            self.across, self.opposite, self.up, self.down, self.up2, self.down2, self.across2
        ):
            copy.wait_send()


class Scatter:
    def __init__(self, net, part, slot, stage, sems):
        self.net, self.part_of, self.slot, self.stage, self.sems = net, part, slot, stage, sems

    def part(self, r, p):
        return self.part_of(self.net.block(r, p))

    def go(self, r):
        net, sems, slot = self.net, self.sems, self.slot
        if r == 2:
            self.across = send(self.part(2, 1), slot(0), sems, 0, net.device(0, 1))
        if r == 1:
            self.up2 = send(self.part(1, 1), slot(2), sems, 2, net.device(1, 0))
            self.up = send(self.part(1, 0), slot(1), sems, 1, net.device(1, 0))
        if r == 3:
            self.down2 = send(self.part(3, 1), slot(4), sems, 4, net.device(3, 0))
            self.down = send(self.part(3, 0), slot(3), sems, 3, net.device(3, 0))

    def middle(self):
        net, sems, slot, stage = self.net, self.sems, self.slot, self.stage
        value = lambda ref: ref[...].astype(F32)
        self.across.wait_recv()
        stage(0)[...] = (value(self.part(2, 0)) + value(slot(0))).astype(BF)
        self.opposite = send(stage(0), slot(5), sems, 5, net.device(2, 0))
        self.up2.wait_recv()
        self.down2.wait_recv()
        total = value(self.part(0, 1)) + value(slot(2)) + value(slot(4))
        stage(1)[...] = total.astype(BF)
        self.across2 = send(stage(1), slot(6), sems, 6, net.device(0, 1))

    def finish(self):
        for copy in (self.up, self.down, self.opposite, self.across2):
            copy.wait_recv()
        for copy in (
            self.across, self.up, self.down, self.up2, self.down2, self.opposite, self.across2
        ):
            copy.wait_send()
        total = self.part(0, 0)[...].astype(F32)
        for i in (1, 3, 5, 6):
            total = total + self.slot(i)[...].astype(F32)
        return total


class WeightGather:
    def __init__(self, chips, other, core, dst, rows, sems, core_sems):
        self.gather = Gather(chips, dst, rows, sems, lambda i: i * 2 + core)
        self.other = other
        self.core_sems = core_sems
        self.copies = []

    def pass_on(self, block):
        i = len(self.copies)
        self.copies.append(send(block, block, self.core_sems, i, self.other))

    def start(self):
        mine = self.gather.at(0, 0)
        self.gather.start(mine)
        self.pass_on(mine)

    def middle(self):
        self.gather.middle(self.pass_on)

    def finish(self):
        self.gather.finish(self.pass_on)
        for copy in self.copies:
            copy.wait()


class WeightScatter:
    def __init__(self, chips, other, core, columns, dw, mine, core_buf, buf, stage, sems, core_sems):
        self.core, self.other, self.core_sems, self.columns = core, other, core_sems, columns
        self.dw, self.mine, self.core_buf = dw, mine, core_buf
        slot = lambda ref: lambda i: ref.at[i, :, columns]
        self.scatter = Scatter(chips, slot(mine), slot(buf), slot(stage), sems)

    def start(self):
        c = self.columns
        self.swap = send(
            self.dw.at[:, 1 - self.core, :, c], self.core_buf.at[:, :, c], self.core_sems, 0, self.other
        )

    def spread(self):
        c = self.columns
        self.swap.wait()

        @pl.loop(0, 8)
        def _(i):
            total = self.dw[i, self.core, :, c].astype(F32) + self.core_buf[i, :, c].astype(F32)
            self.mine[i, :, c] = total.astype(BF)

        for r in (2, 1, 3):
            self.scatter.go(r)

    def middle(self):
        self.scatter.middle()

    def finish(self):
        return self.scatter.finish()


def normed(x):
    average = jnp.mean(x, axis=-1, keepdims=True)
    centered = x - average
    inv = lax.rsqrt(jnp.mean(centered * centered, axis=-1, keepdims=True) + EPSILON)
    return centered * inv, inv


def stream_back(total, grad, stream):
    xhat, inv = normed(stream)
    first = jnp.mean(total, axis=-1, keepdims=True)
    second = jnp.mean(total * xhat, axis=-1, keepdims=True)
    return grad + inv * (total - first - xhat * second)


def nn(a, b):
    return jnp.dot(a, b, preferred_element_type=F32)


def nt(a, b):
    return lax.dot_general(a, b, (((1,), (1,)), ((), ())), preferred_element_type=F32)


def turned(v, cosine, low, high):
    return v * cosine + pltpu.roll(v, 120, 1) * low + pltpu.roll(v, 8, 1) * high


def head_rows(v, h):
    ids = lax.broadcasted_iota(jnp.int32, v.shape, 0)
    return jnp.where((ids < HEAD_DIM) == (h == 0), v, jnp.zeros_like(v))


def head_lanes(v, h):
    ids = lax.broadcasted_iota(jnp.int32, v.shape, 1)
    return jnp.where((ids < HEAD_DIM) == (h == 0), v, jnp.zeros_like(v))


def allowed(first_ref, i):
    keys = (i + 1) * ROWS
    first = first_ref[:, i * ROWS : (i + 1) * ROWS]
    key = lax.broadcasted_iota(jnp.int32, (keys, ROWS), 0)
    query = lax.broadcasted_iota(jnp.int32, (keys, ROWS), 1) + i * ROWS
    return (key >= first) & (key <= query)


def opening(row, lengths):
    second = lengths[:, 0:1]
    third = second + lengths[:, 1:2]
    return jnp.where(row >= third, third, jnp.where(row >= second, second, 0))


def span(i, size):
    return pl.ds(pl.multiple_of(i * size, size), size)


def write_tables(lengths, frequency, cosine, low, high, first):
    @pl.loop(0, 4)
    def _(i):
        row = lax.broadcasted_iota(jnp.int32, (ROWS, 128), 0) + i * ROWS
        angle = (row - opening(row, lengths[...])).astype(F32) * frequency[...]
        sine = jnp.sin(angle)
        lane = lax.rem(lax.broadcasted_iota(jnp.int32, (ROWS, 128), 1), HEAD_DIM)
        r = span(i, ROWS)
        cosine[r] = jnp.cos(angle)
        low[r] = jnp.where(lane < ROT // 2, -sine, 0.0)
        high[r] = jnp.where(lane < ROT // 2, 0.0, sine)

    first[...] = opening(lax.broadcasted_iota(jnp.int32, first.shape, 1), lengths[...])


KEPT = ("q", "k", "v", "q_t", "k_t", "o_t", "lse", "cat", "slope")


class Layer:
    def __init__(self, xg, w, gain, shift, gain_t, shift_t, qkv_b, in_b, tables, first, kept):
        self.xg, self.w, self.gain, self.shift = xg, w, gain, shift
        self.gain_t, self.shift_t, self.qkv_b, self.in_b = gain_t, shift_t, qkv_b, in_b
        self.tables, self.first = tables, first
        for name, ref in zip(KEPT, kept):
            setattr(self, name, ref)

    def project(self, v_t):
        @pl.loop(0, 4)
        def _(i):
            r = span(i, ROWS)
            n1 = (self.xg[r].astype(F32) * self.gain[0:1] + self.shift[0:1]).astype(BF)
            proj = nn(n1, self.w[:, 0:384]) + self.qkv_b[...]
            tables = [table[r] for table in self.tables]
            query = turned(proj[:, 0:128], *tables).astype(BF).astype(F32) * HEAD_DIM**-0.5
            key = turned(proj[:, 128:256], *tables)
            value = proj[:, 256:384]
            for there, flat, across in (
                (query, self.q, self.q_t), (key, self.k, self.k_t), (value, self.v, v_t)
            ):
                flat[r] = there.astype(BF)
                across[:, r] = there.T.astype(BF)

    def attend(self, v_t):
        for i in range(4):
            keys = (i + 1) * ROWS
            r = slice(i * ROWS, keys)
            ok = allowed(self.first, i)
            for h in range(2):
                hs = slice(h * HEAD_DIM, (h + 1) * HEAD_DIM)
                scores = jnp.where(ok, nn(self.k[0:keys], head_rows(self.q_t[:, r], h)), MASKED)
                top = jnp.max(scores, axis=0, keepdims=True)
                weight = jnp.exp(scores - top)
                total = jnp.sum(weight, axis=0, keepdims=True)
                self.o_t[hs, r] = nn(v_t[hs, 0:keys], weight.astype(BF)) / total
                self.lse[h : h + 1, r] = top + jnp.log(total)
            self.cat[r, 0:128] = self.o_t[:, r].T.astype(BF)

    def branch(self, part, block):
        r = span(block, ROWS)
        n2 = (self.xg[r].astype(F32) * self.gain[1:2] + self.shift[1:2]).astype(BF)
        pre = nn(n2, self.w[:, 384:896]) + self.in_b[...]
        bell = 0.5 + 0.5 * lax.erf(pre * 0.5**0.5)
        self.cat[r, 128:640] = (pre * bell).astype(BF)
        self.slope[r] = (bell + pre * jnp.exp(-0.5 * pre * pre) * 0.3989422804014327).astype(BF)
        part[r] = nt(self.cat[r], self.w[:, 896:1536]).astype(BF)

    def back_out(self, gg, da, da_t):
        @pl.loop(0, 4)
        def _(i):
            r = span(i, ROWS)
            cat_grad = nn(gg[r], self.w[:, 896:1536])
            da[r] = cat_grad[:, 0:128].astype(BF)
            da_t[:, r] = cat_grad[:, 0:128].T.astype(BF)
            self.slope[r] = (cat_grad[:, 128:640] * self.slope[r].astype(F32)).astype(BF)

    def attend_back(self, blocks, da, da_t, dk, dv, dq_t):
        for i in blocks:
            keys = (i + 1) * ROWS
            r = slice(i * ROWS, keys)
            ok = allowed(self.first, i)
            for h in range(2):
                hs = slice(h * HEAD_DIM, (h + 1) * HEAD_DIM)
                scores = nn(self.k[0:keys], head_rows(self.q_t[:, r], h))
                prob = jnp.exp(jnp.where(ok, scores, MASKED) - self.lse[h : h + 1, r])
                centre = jnp.sum(da_t[hs, r].astype(F32) * self.o_t[hs, r], axis=0, keepdims=True)
                prob_grad = nn(self.v[0:keys], head_rows(da_t[:, r], h))
                score_grad = (prob * (prob_grad - centre)).astype(BF)
                dv[0:keys] += nn(prob.astype(BF), head_lanes(da[r], h))
                dk[0:keys] += nn(score_grad, head_lanes(self.q[r], h))
                dq_t[hs, r] = nn(self.k_t[hs, 0:keys], score_grad) * HEAD_DIM**-0.5

    def back_in(self, part, block, dk, dv, dq_t, proj_grad, cols, small, where_cols, where_small):
        r = span(block, ROWS)
        tables = self.tables[0][r], -self.tables[1][r], -self.tables[2][r]
        proj_grad[r, 0:128] = turned(dq_t[:, r].T, *tables).astype(BF)
        proj_grad[r, 128:256] = turned(dk[r], *tables).astype(BF)
        proj_grad[r, 256:384] = dv[r].astype(BF)
        pg, hg = proj_grad[r], self.slope[r]
        g1 = nt(pg, self.w[:, 0:384])
        g2 = nt(hg, self.w[:, 384:896])
        part[r] = (g1 * self.gain[0:1] + g2 * self.gain[1:2]).astype(BF)
        for grad, n, at in ((pg, 3, 0), (hg, 4, 3)):
            sums = jnp.sum(grad.astype(F32), axis=0, keepdims=True)
            for c in range(n):
                row = where_cols + at + c
                cols[row : row + 1] += sums[:, c * 128 : (c + 1) * 128]
        x = self.xg[r].astype(F32)
        for j, sums in enumerate((g1 * x, g2 * x, g1, g2)):
            row = where_small + j
            small[row : row + 1] += jnp.sum(sums, axis=0, keepdims=True)

    def grads(self, dw, gg, proj_grad, which):
        @pl.loop(0, 4)
        def _(j):
            c = span(j, ROWS)
            chips = pl.ds(j * 2, 2)

            def put(left, right, columns):
                dw[chips, :, :, columns] = nn(left, right).astype(BF).reshape(2, 2, 64, right.shape[1])

            x_t = self.xg[:, c].T.astype(F32)
            if "q" in which:
                n1_t = (x_t * self.gain_t[c, 0:1] + self.shift_t[c, 0:1]).astype(BF)
                put(n1_t, proj_grad[...], slice(0, 384))
            if "f" in which:
                n2_t = (x_t * self.gain_t[c, 1:2] + self.shift_t[c, 1:2]).astype(BF)
                put(n2_t, self.slope[...], slice(384, 896))
                put(gg[:, c].T, self.cat[...], slice(896, 1536))


INPUTS = (
    "tokens", "cotangent", "lengths", "frequency", "qkv_w", "in_w", "dense_w", "out_w",
    "gain", "shift", "gain_t", "shift_t", "qkv_b", "in_b", "out_b",
)
OUTPUTS = ("output", "input_grad", "dw_out", "qkv_b_grad", "in_b_grad", "bias_grad", "gain_grad", "shift_grad")


def scratch_list():
    n = 1024
    v = pltpu.VMEM
    items = {}
    for l in "01":
        items["xg" + l] = v((n, n), BF)
        items["gg" + l] = v((n, n), BF)
        items["w" + l] = v((n, 1536), BF)
        items["core_buf" + l] = v((8, 64, 1536), BF)
        items["chip_buf" + l] = v((7, 64, 1536), BF)
        for name in ("q", "k", "v"):
            items[name + l] = v((n, 128), BF)
        for name in ("q_t", "k_t"):
            items[name + l] = v((128, n), BF)
        items["o_t" + l] = v((128, n), F32)
        items["lse" + l] = v((8, n), F32)
        items["cat" + l] = v((n, 640), BF)
        items["slope" + l] = v((n, 512), BF)
        items["ws" + l] = DMA((2, 7))
        items["cs" + l] = DMA((2, 8))
        items["rs" + l] = DMA((2, 7))
        items["bs" + l] = DMA((2, 7))
        items["ts" + l] = DMA((2, 7))
        items["gs" + l] = DMA((2, 7))
        for name in ("fbuf", "bbuf"):
            items[name + l] = v((7, 128, n), BF)
        for name in ("fstage", "bstage"):
            items[name + l] = v((2, 128, n), BF)
    for l in ("1", "a", "b"):
        items["ds" + l] = DMA((2, 7))
        items["dc" + l] = DMA((2, 1))
    items["v_t"] = v((128, n), BF)
    items["part"] = v((n, n), BF)
    items["part_out"] = v((n, n), BF)
    items["dw"] = v((8, 2, 64, 1536), BF)
    items["mine"] = v((8, 64, 1536), BF)
    items["chip_stage"] = v((2, 64, 1536), BF)
    for name in ("cosine", "low", "high"):
        items[name] = v((n, 128), F32)
    items["first"] = v((1, n), jnp.int32)
    items["da"] = v((n, 128), BF)
    items["da_t"] = v((128, n), BF)
    items["proj_grad"] = v((n, 384), BF)
    items["dk"] = v((n, 128), F32)
    items["dv"] = v((n, 128), F32)
    items["dq_t"] = v((128, n), F32)
    items["stream1"] = v((128, n), F32)
    items["grad1"] = v((128, n), F32)
    items["small"] = v((16, n), F32)
    items["small_buf"] = v((7, 16, 128), F32)
    items["both"] = v((32, 128), F32)
    items["both_buf"] = v((15, 32, 128), F32)
    items["spread"] = v((8, 16, 128), F32)
    items["ss"] = DMA((2, 7))
    items["os"] = DMA((2, 15))
    items["es"] = DMA((2, 7))
    return items


DMA = pltpu.SemaphoreType.DMA


class Refs:
    pass


def whole_kernel(names, *refs):
    z = Refs()
    for name, ref in zip(names, refs):
        setattr(z, name, ref)
    d, t, core, tensor, chips = place()
    other = (d + 1 - 2 * core, t)
    mine_rows = span(t, 128)
    shard = span(d, 64)
    steps = [(r, p) for r in range(4) for p in range(2) if r or p]
    others = [(lax.rem(d + k, 16), t) for k in range(1, 16)]

    for l, w in enumerate((z.w0, z.w1)):
        w[shard, 0:384] = z.qkv_w[l]
        w[shard, 384:896] = z.in_w[l]
        w[shard, 896:1024] = z.dense_w[l]
        w[shard, 1024:1536] = z.out_w[l]
    z.xg0[mine_rows] = normed(z.tokens[...].astype(F32))[0].astype(BF)
    z.gg1[mine_rows] = z.cotangent[...]
    z.small[...] = jnp.zeros_like(z.small)
    z.both[...] = jnp.zeros_like(z.both)
    z.small[9:10] = jnp.sum(z.cotangent[...].astype(F32), axis=0, keepdims=True)

    greet([tensor.device(*s) for s in steps] + others)
    rows0 = Gather(tensor, z.xg0, 128, z.ts0)
    weights0 = WeightGather(chips, other, core, z.w0, 64, z.ws0, z.cs0)
    rows0.start(rows0.at(0, 0))
    weights0.start()
    write_tables(z.lengths, z.frequency, z.cosine, z.low, z.high, z.first)
    rows0.middle()
    weights0.middle()
    rows0.finish()
    weights0.finish()
    cotangent = Gather(tensor, z.gg1, 128, z.gs1)
    cotangent.start(cotangent.at(0, 0))
    weights1 = WeightGather(chips, other, core, z.w1, 64, z.ws1, z.cs1)
    weights1.start()

    tables = (z.cosine, z.low, z.high)
    layers = [
        Layer(
            getattr(z, "xg%d" % l), getattr(z, "w%d" % l), z.gain.at[l], z.shift.at[l],
            z.gain_t.at[l], z.shift_t.at[l], z.qkv_b.at[l], z.in_b.at[l], tables, z.first,
            [getattr(z, "%s%d" % (name, l)) for name in KEPT],
        )
        for l in range(2)
    ]

    def tensor_scatter(part, buf, stage, sems):
        return Scatter(
            tensor, lambda i: part.at[span(i, 128)], lambda i: buf.at[i], lambda i: stage.at[i], sems
        )

    layers[0].project(z.v_t)
    layers[0].attend(z.v_t)
    cotangent.middle()
    weights1.middle()
    sum0 = tensor_scatter(z.part, z.fbuf0, z.fstage0, z.rs0)
    for r in (2, 1, 3, 0):
        layers[0].branch(z.part, lax.rem(tensor.ring + r, 4))
        sum0.go(r)
    sum0.middle()
    weights1.finish()
    stream = z.tokens[...].astype(F32) + sum0.finish() + z.out_b[0:1]
    z.stream1[...] = stream
    z.xg1[mine_rows] = normed(stream)[0].astype(BF)
    rows1 = Gather(tensor, z.xg1, 128, z.ts1)
    rows1.start(rows1.at(0, 0))
    rows1.middle()
    rows1.finish()

    layers[1].project(z.v_t)
    layers[1].attend(z.v_t)
    sum1 = tensor_scatter(z.part_out, z.fbuf1, z.fstage1, z.rs1)
    for r in (2, 1, 3, 0):
        layers[1].branch(z.part_out, lax.rem(tensor.ring + r, 4))
        sum1.go(r)

    def weight_scatter(tag, columns, l, sems, core_sems):
        return WeightScatter(
            chips, other, core, columns, z.dw, z.mine, getattr(z, "core_buf%d" % l),
            getattr(z, "chip_buf%d" % l), z.chip_stage, sems, core_sems,
        )

    z.dk[...] = jnp.zeros_like(z.dk)
    z.dv[...] = jnp.zeros_like(z.dv)
    cotangent.finish()
    layers[1].back_out(z.gg1, z.da, z.da_t)
    layers[1].attend_back((0, 1, 2), z.da, z.da_t, z.dk, z.dv, z.dq_t)
    sum1.middle()
    layers[1].attend_back((3,), z.da, z.da_t, z.dk, z.dv, z.dq_t)
    back1 = tensor_scatter(z.part, z.bbuf1, z.bstage1, z.bs1)
    for r in (2, 1, 3, 0):
        layers[1].back_in(
            z.part, lax.rem(tensor.ring + r, 4), z.dk, z.dv, z.dq_t, z.proj_grad, z.both, z.small, 23, 4
        )
        back1.go(r)
    layers[1].grads(z.dw, z.gg1, z.proj_grad, "qf")
    weights_back1 = weight_scatter("1", slice(0, 1536), 1, z.ds1, z.dc1)
    weights_back1.start()
    back1.middle()
    weights_back1.spread()
    grad = stream_back(back1.finish(), z.cotangent[...].astype(F32), z.stream1[...])
    z.grad1[...] = grad
    z.gg0[mine_rows] = grad.astype(BF)
    grads0 = Gather(tensor, z.gg0, 128, z.gs0)
    grads0.start(grads0.at(0, 0))
    z.small[8:9] = jnp.sum(grad, axis=0, keepdims=True)
    z.dk[...] = jnp.zeros_like(z.dk)
    z.dv[...] = jnp.zeros_like(z.dv)
    grads0.middle()
    weights_back1.middle()
    z.output[...] = (z.stream1[...] + sum1.finish() + z.out_b[1:2]).astype(BF)
    grads0.finish()

    layers[0].back_out(z.gg0, z.da, z.da_t)
    z.dw_out[1] = weights_back1.finish()
    layers[0].grads(z.dw, z.gg0, z.proj_grad, "f")
    weights_back0 = weight_scatter("a", slice(384, 1536), 0, z.dsa, z.dca)
    weights_back0.start()
    layers[0].attend_back((0, 1), z.da, z.da_t, z.dk, z.dv, z.dq_t)
    weights_back0.spread()
    layers[0].attend_back((2, 3), z.da, z.da_t, z.dk, z.dv, z.dq_t)
    back0 = tensor_scatter(z.part, z.bbuf0, z.bstage0, z.bs0)
    for r in (2, 1, 3, 0):
        layers[0].back_in(
            z.part, lax.rem(tensor.ring + r, 4), z.dk, z.dv, z.dq_t, z.proj_grad, z.both, z.small, 16, 0
        )
        back0.go(r)
    small = [
        send(z.small.at[:, span(tensor.block(*s), 128)], z.small_buf.at[i], z.ss, i, tensor.device(*s))
        for i, s in enumerate(steps)
    ]
    layers[0].grads(z.dw, z.gg0, z.proj_grad, "q")
    weights_last = weight_scatter("b", slice(0, 384), 0, z.dsb, z.dcb)
    weights_last.start()
    weights_back0.middle()
    back0.middle()
    weights_last.spread()
    for c in small:
        c.wait()
    total = z.small[:, span(t, 128)]
    for i in range(7):
        total = total + z.small_buf[i]
    z.both[0:16] = total
    both = [send(z.both, z.both_buf.at[i], z.os, i, p) for i, p in enumerate(others)]
    weights_last.middle()
    for c in both:
        c.wait()
    total = z.both[...]
    for i in range(15):
        total = total + z.both_buf[i]
    z.spread[t] = total[0:16]
    spread = [
        send(z.spread.at[t], z.spread.at[t], z.es, i, tensor.device(*s)) for i, s in enumerate(steps)
    ]
    for l in range(2):
        for c in range(3):
            row = 16 + 7 * l + c
            z.qkv_b_grad[l, c : c + 1] = total[row : row + 1]
        for c in range(4):
            row = 19 + 7 * l + c
            z.in_b_grad[l : l + 1, c * 128 : (c + 1) * 128] = total[row : row + 1]
    z.dw_out[0, :, 384:1536] = weights_back0.finish()
    z.input_grad[...] = stream_back(back0.finish(), z.grad1[...], z.tokens[...].astype(F32))
    z.dw_out[0, :, 0:384] = weights_last.finish()
    for c in spread:
        c.wait()
    for i in range(8):
        lanes = slice(i * 128, (i + 1) * 128)
        for l in range(2):
            z.gain_grad[l, :, lanes] = z.spread[i, 4 * l : 4 * l + 2]
            z.shift_grad[l, :, lanes] = z.spread[i, 4 * l + 2 : 4 * l + 4]
        z.bias_grad[:, lanes] = z.spread[i, 8:10]


def local(
    tokens,
    lengths,
    qkv_weight,
    qkv_bias,
    dense_weight,
    dense_bias,
    fc_in_weight,
    fc_in_bias,
    fc_out_weight,
    fc_out_bias,
    norm_gain,
    norm_bias,
    cotangent,
):
    lane = np.arange(128) % HEAD_DIM
    half_rot = ROT // 2
    base = 10000.0 ** (-(2.0 * jnp.arange(half_rot, dtype=F32)) / ROT)
    frequency = jnp.where(jnp.asarray(lane < ROT), base[lane % half_rot], 0.0)[None, :]
    gain = norm_gain.astype(F32)
    shift = norm_bias.astype(F32)
    inputs = (
        tokens,
        cotangent,
        lengths,
        frequency,
        qkv_weight.reshape(2, 64, 384),
        fc_in_weight,
        dense_weight.swapaxes(1, 2),
        fc_out_weight.swapaxes(1, 2),
        gain,
        shift,
        gain.swapaxes(1, 2),
        shift.swapaxes(1, 2),
        qkv_bias.astype(F32).reshape(2, 1, 384),
        fc_in_bias.astype(F32).reshape(2, 1, 512),
        dense_bias.astype(F32) + fc_out_bias.astype(F32),
    )
    s = jax.ShapeDtypeStruct
    shapes = (
        s((128, 1024), BF),
        s((128, 1024), F32),
        s((2, 64, 1536), F32),
        s((2, 3, 128), F32),
        s((2, 512), F32),
        s((2, 1024), F32),
        s((2, 2, 1024), F32),
        s((2, 2, 1024), F32),
    )
    scratch = scratch_list()
    names = INPUTS + OUTPUTS + tuple(scratch)
    output, input_grad, dw, qkv_b_grad, in_b_grad, bias_grad, gain_grad, shift_grad = pl.pallas_call(
        lambda *refs: whole_kernel(names, *refs),
        out_shape=shapes,
        in_specs=[VM] * len(inputs),
        out_specs=(VM,) * len(shapes),
        scratch_shapes=list(scratch.values()),
        compiler_params=pltpu.CompilerParams(
            collective_id=1, has_side_effects=True, vmem_limit_bytes=63 * 2**20
        ),
        cost_estimate=pl.CostEstimate(flops=0, bytes_accessed=600_000_000, transcendentals=0),
        name="layers_forward_and_backward",
    )(*inputs)
    return (
        output,
        input_grad,
        dw[:, :, 0:384].reshape(2, 64, 3, 128),
        qkv_b_grad,
        dw[:, :, 896:1024].swapaxes(1, 2),
        bias_grad,
        dw[:, :, 384:896],
        in_b_grad,
        dw[:, :, 1024:1536].swapaxes(1, 2),
        bias_grad,
        gain_grad,
        shift_grad,
    )


def solution(mesh):
    return jax.shard_map(
        local,
        mesh=mesh,
        in_specs=(
            P(("dp", "tensor"), None),
            P("dp", None),
            P(None, "dp", None, "tensor"),
            P(None, None, "tensor"),
            P(None, "tensor", "dp"),
            P(),
            P(None, "dp", "tensor"),
            P(None, "tensor"),
            P(None, "tensor", "dp"),
            P(),
            P(),
            P(),
            P(("dp", "tensor"), None),
        ),
        out_specs=(
            P(("dp", "tensor"), None),
            P(("dp", "tensor"), None),
            P(None, "dp", None, "tensor"),
            P(None, None, "tensor"),
            P(None, "tensor", "dp"),
            P(),
            P(None, "dp", "tensor"),
            P(None, "tensor"),
            P(None, "tensor", "dp"),
            P(),
            P(),
            P(),
        ),
        check_vma=False,
    )
```

```python
import jax
import jax.numpy as jnp
import numpy as np
from jax import lax
from jax.experimental import pallas as pl
from jax.experimental.pallas import tpu as pltpu
from jax.sharding import PartitionSpec as P

MESH = pl.DeviceIdType.MESH
HEAD_DIM = 64
ROT = 16
EPSILON = 1e-05
MASKED = -1000000000.0
ROWS = 256
BF = jnp.bfloat16
F32 = jnp.float32
VM = pl.BlockSpec(memory_space=pltpu.VMEM)


class Net:
    def __init__(self, ring, pair, index, device):
        self.ring, self.pair, self.index_of, self.device_of = ring, pair, index, device

    def block(self, r, p):
        return self.index_of(lax.rem(self.ring + r, 4), lax.rem(self.pair + p, 2))

    def device(self, r, p):
        return self.device_of(self.block(r, p))


def place():
    d = lax.axis_index("dp")
    t = lax.axis_index("tensor")
    core = lax.rem(d, 2)
    tensor = Net(t // 2, lax.rem(t, 2), lambda r, p: r * 2 + p, lambda i: (d, i))
    chips = Net(lax.rem(d // 2, 4), d // 8, lambda r, p: p * 4 + r, lambda i: (i * 2 + core, t))
    return d, t, core, tensor, chips


PEERS = [(1, 0), (3, 0), (2, 0), (0, 1)]


def greet(devices):
    barrier = pltpu.get_barrier_semaphore()
    for device in devices:
        pl.semaphore_signal(barrier, inc=1, device_id=device, device_id_type=MESH)
    pl.semaphore_wait(barrier, len(devices))


def send(src, dst, sems, i, device):
    copy = pltpu.make_async_remote_copy(
        src_ref=src,
        dst_ref=dst,
        send_sem=sems.at[0, i],
        recv_sem=sems.at[1, i],
        device_id=device,
        device_id_type=MESH,
    )
    copy.start()
    return copy


class Gather:
    def __init__(self, net, block, rows, sems):
        self.net, self.block, self.rows, self.sems, self.copies = net, block, rows, sems, []

    def at(self, r, p):
        return self.block(self.net.block(r, p))

    def piece(self, r, p, c, n):
        return self.at(r, p).at[pl.ds(c * self.rows // n, self.rows // n)]

    def send(self, block, r, p):
        copy = send(block, block, self.sems, len(self.copies), self.net.device(r, p))
        self.copies.append(copy)
        return copy

    def start(self):
        self.across = self.send(self.at(0, 0), 0, 1)
        self.first = []
        for c in range(2):
            self.first.append((self.send(self.piece(0, 0, c, 4), 1, 0), 1, 3, c))
            self.first.append((self.send(self.piece(0, 0, 2 + c, 4), 3, 0), 3, 1, 2 + c))
        self.up = self.send(self.piece(0, 0, 1, 2), 1, 0)
        self.down = self.send(self.piece(0, 0, 0, 2), 3, 0)

    def middle(self, seen=lambda block: None):
        self.second = []
        for copy, ahead, behind, c in self.first:
            copy.wait_recv()
            self.second.append((self.send(self.piece(behind, 0, c, 4), ahead, 0), c))
        self.across.wait_recv()
        self.up2 = self.send(self.at(0, 1), 1, 0)
        self.down2 = self.send(self.at(0, 1), 3, 0)
        seen(self.at(0, 1))

    def last(self, seen=lambda block: None):
        self.third = []
        for copy, c in self.second:
            copy.wait_recv()
            self.third.append(self.send(self.piece(2, 0, c, 4), 0, 1))
        seen(self.at(2, 0))

    def finish(self, seen=lambda block: None):
        for copies, r, p in (
            ([self.up], 3, 0), ([self.down], 1, 0), ([self.up2], 3, 1), ([self.down2], 1, 1), (self.third, 2, 1)
        ):
            for copy in copies:
                copy.wait_recv()
            seen(self.at(r, p))
        for copy in self.copies:
            copy.wait_send()


def add(ref, *others):
    total = ref[...].astype(F32)
    for other in others:
        total = total + other[...].astype(F32)
    ref[...] = total.astype(BF)


class Scatter:
    def __init__(self, net, part, slot, rows, sems):
        self.net, self.part_of, self.slot, self.rows, self.sems = net, part, slot, rows, sems
        self.copies = []

    def part(self, r, p):
        return self.part_of(self.net.block(r, p))

    def half(self, ref, c):
        return ref.at[pl.ds(c * self.rows // 2, self.rows // 2)]

    def send(self, src, dst, r, p):
        copy = send(src, dst, self.sems, len(self.copies), self.net.device(r, p))
        self.copies.append(copy)
        return copy

    def go(self, r):
        if r == 2:
            self.across = self.send(self.part(2, 1), self.slot(0), 0, 1)
        if r == 1:
            self.up2 = self.send(self.part(1, 1), self.slot(2), 1, 0)
            self.up = self.send(self.half(self.part(1, 0), 0), self.half(self.slot(1), 0), 1, 0)
        if r == 3:
            self.down2 = self.send(self.part(3, 1), self.slot(4), 3, 0)
            self.down = self.send(self.half(self.part(3, 0), 1), self.half(self.slot(3), 1), 3, 0)

    def middle(self):
        self.across.wait_recv()
        add(self.part(2, 0), self.slot(0))
        self.far_down = self.send(self.half(self.part(2, 0), 0), self.half(self.slot(5), 0), 3, 0)
        self.far_up = self.send(self.half(self.part(2, 0), 1), self.half(self.slot(5), 1), 1, 0)
        self.up2.wait_recv()
        self.down2.wait_recv()
        add(self.part(0, 1), self.slot(2), self.slot(4))
        self.across2 = self.send(self.part(0, 1), self.slot(6), 0, 1)

    def last(self):
        self.far_down.wait_recv()
        block = self.half(self.part(3, 0), 0)
        add(block, self.half(self.slot(5), 0))
        self.near_down = self.send(block, self.half(self.slot(3), 0), 3, 0)
        self.far_up.wait_recv()
        block = self.half(self.part(1, 0), 1)
        add(block, self.half(self.slot(5), 1))
        self.near_up = self.send(block, self.half(self.slot(1), 1), 1, 0)

    def finish(self):
        for copy in (self.up, self.down, self.across2, self.near_down, self.near_up):
            copy.wait_recv()
        for copy in self.copies:
            copy.wait_send()
        total = self.part(0, 0)[...].astype(F32)
        for i in (1, 3, 6):
            total = total + self.slot(i)[...].astype(F32)
        return total


class WeightGather:
    def __init__(self, chips, other, core, columns, dst, sems, core_sems):
        block = lambda i: dst.at[span(i * 2 + core, 64), columns]
        self.gather = Gather(chips, block, 64, sems)
        self.other = other
        self.core_sems = core_sems
        self.copies = []

    def pass_on(self, block):
        i = len(self.copies)
        self.copies.append(send(block, block, self.core_sems, i, self.other))

    def start(self):
        self.gather.start()
        self.pass_on(self.gather.at(0, 0))

    def middle(self):
        self.gather.middle(self.pass_on)

    def last(self):
        self.gather.last(self.pass_on)

    def finish(self):
        self.gather.finish(self.pass_on)
        for copy in self.copies:
            copy.wait()


class WeightScatter:
    def __init__(self, chips, other, core, columns, dw, mine, core_buf, buf, sems, core_sems):
        self.core, self.other, self.core_sems, self.columns = core, other, core_sems, columns
        self.dw, self.mine, self.core_buf = dw, mine, core_buf
        slot = lambda ref: lambda i: ref.at[i, :, columns]
        self.scatter = Scatter(chips, slot(mine), slot(buf), 64, sems)

    def start(self):
        c = self.columns
        self.swap = send(
            self.dw.at[:, 1 - self.core, :, c], self.core_buf.at[:, :, c], self.core_sems, 0, self.other
        )

    def spread(self):
        c = self.columns
        self.swap.wait()

        @pl.loop(0, 8)
        def _(i):
            total = self.dw[i, self.core, :, c].astype(F32) + self.core_buf[i, :, c].astype(F32)
            self.mine[i, :, c] = total.astype(BF)

        for r in (2, 1, 3):
            self.scatter.go(r)

    def middle(self):
        self.scatter.middle()

    def last(self):
        self.scatter.last()

    def finish(self):
        return self.scatter.finish()


def normed(x):
    average = jnp.mean(x, axis=-1, keepdims=True)
    centered = x - average
    inv = lax.rsqrt(jnp.mean(centered * centered, axis=-1, keepdims=True) + EPSILON)
    return centered * inv, inv


def stream_back(total, grad, stream):
    xhat, inv = normed(stream)
    first = jnp.mean(total, axis=-1, keepdims=True)
    second = jnp.mean(total * xhat, axis=-1, keepdims=True)
    return grad + inv * (total - first - xhat * second)


def nn(a, b):
    return jnp.dot(a, b, preferred_element_type=F32)


def nt(a, b):
    return lax.dot_general(a, b, (((1,), (1,)), ((), ())), preferred_element_type=F32)


def turned(v, cosine, low, high):
    return v * cosine + pltpu.roll(v, 120, 1) * low + pltpu.roll(v, 8, 1) * high


def head_rows(v, h):
    ids = lax.broadcasted_iota(jnp.int32, v.shape, 0)
    return jnp.where((ids < HEAD_DIM) == (h == 0), v, jnp.zeros_like(v))


def head_lanes(v, h):
    ids = lax.broadcasted_iota(jnp.int32, v.shape, 1)
    return jnp.where((ids < HEAD_DIM) == (h == 0), v, jnp.zeros_like(v))


def allowed(first_ref, i):
    keys = (i + 1) * ROWS
    first = first_ref[:, i * ROWS : (i + 1) * ROWS]
    key = lax.broadcasted_iota(jnp.int32, (keys, ROWS), 0)
    query = lax.broadcasted_iota(jnp.int32, (keys, ROWS), 1) + i * ROWS
    return (key >= first) & (key <= query)


def opening(row, lengths):
    second = lengths[:, 0:1]
    third = second + lengths[:, 1:2]
    return jnp.where(row >= third, third, jnp.where(row >= second, second, 0))


def span(i, size):
    return pl.ds(pl.multiple_of(i * size, size), size)


def write_tables(lengths, frequency, cosine, low, high, first):
    @pl.loop(0, 4)
    def _(i):
        row = lax.broadcasted_iota(jnp.int32, (ROWS, 128), 0) + i * ROWS
        angle = (row - opening(row, lengths[...])).astype(F32) * frequency[...]
        sine = jnp.sin(angle)
        lane = lax.rem(lax.broadcasted_iota(jnp.int32, (ROWS, 128), 1), HEAD_DIM)
        r = span(i, ROWS)
        cosine[r] = jnp.cos(angle)
        low[r] = jnp.where(lane < ROT // 2, -sine, 0.0)
        high[r] = jnp.where(lane < ROT // 2, 0.0, sine)

    first[...] = opening(lax.broadcasted_iota(jnp.int32, first.shape, 1), lengths[...])


KEPT = ("q", "k", "v", "q_t", "k_t", "o_t", "lse", "cat", "slope")


class Layer:
    def __init__(self, xg, w, norms, norms_t, qkv_b, in_b, tables, first, kept):
        self.xg, self.w, self.norms, self.norms_t = xg, w, norms, norms_t
        self.qkv_b, self.in_b = qkv_b, in_b
        self.tables, self.first = tables, first
        for name, ref in zip(KEPT, kept):
            setattr(self, name, ref)

    def project(self, v_t):
        @pl.loop(0, 4)
        def _(i):
            r = span(i, ROWS)
            n1 = (self.xg[r].astype(F32) * self.norms[0:1] + self.norms[2:3]).astype(BF)
            proj = nn(n1, self.w[:, 0:384]) + self.qkv_b[...]
            tables = [table[r] for table in self.tables]
            query = turned(proj[:, 0:128], *tables).astype(BF).astype(F32) * HEAD_DIM**-0.5
            key = turned(proj[:, 128:256], *tables)
            value = proj[:, 256:384]
            for there, flat, across in (
                (query, self.q, self.q_t), (key, self.k, self.k_t), (value, self.v, v_t)
            ):
                flat[r] = there.astype(BF)
                across[:, r] = there.T.astype(BF)

    def attend(self, v_t):
        for i in range(4):
            keys = (i + 1) * ROWS
            r = slice(i * ROWS, keys)
            ok = allowed(self.first, i)
            for h in range(2):
                hs = slice(h * HEAD_DIM, (h + 1) * HEAD_DIM)
                scores = jnp.where(ok, nn(self.k[0:keys], head_rows(self.q_t[:, r], h)), MASKED)
                top = jnp.max(scores, axis=0, keepdims=True)
                weight = jnp.exp(scores - top)
                total = jnp.sum(weight, axis=0, keepdims=True)
                self.o_t[hs, r] = nn(v_t[hs, 0:keys], weight.astype(BF)) / total
                self.lse[h : h + 1, r] = top + jnp.log(total)
            self.cat[r, 0:128] = self.o_t[:, r].T.astype(BF)

    def branch(self, part, block):
        r = span(block, ROWS)
        n2 = (self.xg[r].astype(F32) * self.norms[1:2] + self.norms[3:4]).astype(BF)
        pre = nn(n2, self.w[:, 384:896]) + self.in_b[...]
        bell = 0.5 + 0.5 * lax.erf(pre * 0.5**0.5)
        self.cat[r, 128:640] = (pre * bell).astype(BF)
        self.slope[r] = (bell + pre * jnp.exp(-0.5 * pre * pre) * 0.3989422804014327).astype(BF)
        part[r] = nt(self.cat[r], self.w[:, 896:1536]).astype(BF)

    def back_out(self, gg, da, da_t):
        @pl.loop(0, 4)
        def _(i):
            r = span(i, ROWS)
            cat_grad = nn(gg[r], self.w[:, 896:1536])
            da[r] = cat_grad[:, 0:128].astype(BF)
            da_t[:, r] = cat_grad[:, 0:128].T.astype(BF)
            self.slope[r] = (cat_grad[:, 128:640] * self.slope[r].astype(F32)).astype(BF)

    def attend_back(self, blocks, da, da_t, dk, dv, dq_t):
        for i in blocks:
            keys = (i + 1) * ROWS
            r = slice(i * ROWS, keys)
            ok = allowed(self.first, i)
            for h in range(2):
                hs = slice(h * HEAD_DIM, (h + 1) * HEAD_DIM)
                scores = nn(self.k[0:keys], head_rows(self.q_t[:, r], h))
                prob = jnp.exp(jnp.where(ok, scores, MASKED) - self.lse[h : h + 1, r])
                centre = jnp.sum(da_t[hs, r].astype(F32) * self.o_t[hs, r], axis=0, keepdims=True)
                prob_grad = nn(self.v[0:keys], head_rows(da_t[:, r], h))
                score_grad = (prob * (prob_grad - centre)).astype(BF)
                dv[0:keys] += nn(prob.astype(BF), head_lanes(da[r], h))
                dk[0:keys] += nn(score_grad, head_lanes(self.q[r], h))
                dq_t[hs, r] = nn(self.k_t[hs, 0:keys], score_grad) * HEAD_DIM**-0.5

    def back_in(self, part, block, dk, dv, dq_t, proj_grad, cols, small, where_cols, where_small):
        r = span(block, ROWS)
        tables = self.tables[0][r], -self.tables[1][r], -self.tables[2][r]
        proj_grad[r, 0:128] = turned(dq_t[:, r].T, *tables).astype(BF)
        proj_grad[r, 128:256] = turned(dk[r], *tables).astype(BF)
        proj_grad[r, 256:384] = dv[r].astype(BF)
        pg, hg = proj_grad[r], self.slope[r]
        g1 = nt(pg, self.w[:, 0:384])
        g2 = nt(hg, self.w[:, 384:896])
        part[r] = (g1 * self.norms[0:1] + g2 * self.norms[1:2]).astype(BF)
        for grad, n, at in ((pg, 3, 0), (hg, 4, 3)):
            sums = jnp.sum(grad.astype(F32), axis=0, keepdims=True)
            for c in range(n):
                row = where_cols + at + c
                cols[row : row + 1] += sums[:, c * 128 : (c + 1) * 128]
        x = self.xg[r].astype(F32)
        for j, sums in enumerate((g1 * x, g2 * x, g1, g2)):
            row = where_small + j
            small[row : row + 1] += jnp.sum(sums, axis=0, keepdims=True)

    def grads(self, dw, gg, proj_grad, which):
        @pl.loop(0, 4)
        def _(j):
            c = span(j, ROWS)
            chips = pl.ds(j * 2, 2)

            def put(left, right, columns):
                dw[chips, :, :, columns] = nn(left, right).astype(BF).reshape(2, 2, 64, right.shape[1])

            x_t = self.xg[:, c].T.astype(F32)
            if "q" in which:
                n1_t = (x_t * self.norms_t[c, 0:1] + self.norms_t[c, 2:3]).astype(BF)
                put(n1_t, proj_grad[...], slice(0, 384))
            if "f" in which:
                n2_t = (x_t * self.norms_t[c, 1:2] + self.norms_t[c, 3:4]).astype(BF)
                put(n2_t, self.slope[...], slice(384, 896))
                put(gg[:, c].T, self.cat[...], slice(896, 1536))


INPUTS = (
    "tokens", "cotangent", "lengths", "frequency", "qkv_w", "in_w", "dense_w", "out_w",
    "gain", "shift", "qkv_b", "in_b", "dense_b", "out_b",
)
OUTPUTS = ("output", "input_grad", "dw_out", "qkv_b_grad", "in_b_grad", "bias_grad", "gain_grad", "shift_grad")


def scratch_list():
    n = 1024
    v = pltpu.VMEM
    items = {}
    for l in "01":
        items["xg" + l] = v((n, n), BF)
        items["gg" + l] = v((n, n), BF)
        items["w" + l] = v((n, 1536), BF)
        items["core_buf" + l] = v((8, 64, 1536), BF)
        items["chip_buf" + l] = v((7, 64, 1536), BF)
        for name in ("q", "k", "v"):
            items[name + l] = v((n, 128), BF)
        for name in ("q_t", "k_t"):
            items[name + l] = v((128, n), BF)
        items["o_t" + l] = v((128, n), F32)
        items["lse" + l] = v((8, n), F32)
        items["cat" + l] = v((n, 640), BF)
        items["slope" + l] = v((n, 512), BF)
        items["bs" + l] = DMA((2, 10))
        items["ts" + l] = DMA((2, 17))
        for name in ("fbuf", "bbuf"):
            items[name + l] = v((7, 128, n), BF)
    for l in ("q", "f", "1"):
        items["ws" + l] = DMA((2, 17))
        items["cs" + l] = DMA((2, 8))
    for l in "0ab":
        items["rs" + l] = DMA((2, 10))
        items["gs" + l] = DMA((2, 17))
    for l in ("1", "a", "b"):
        items["ds" + l] = DMA((2, 10))
        items["dc" + l] = DMA((2, 1))
    items["v_t"] = v((128, n), BF)
    items["part"] = v((n, n), BF)
    items["part_out"] = v((n, n), BF)
    items["dw"] = v((8, 2, 64, 1536), BF)
    items["mine"] = v((8, 64, 1536), BF)
    for name in ("cosine", "low", "high"):
        items[name] = v((n, 128), F32)
    items["first"] = v((1, n), jnp.int32)
    items["da"] = v((n, 128), BF)
    items["da_t"] = v((128, n), BF)
    items["proj_grad"] = v((n, 384), BF)
    items["dk"] = v((n, 128), F32)
    items["dv"] = v((n, 128), F32)
    items["dq_t"] = v((128, n), F32)
    items["stream1"] = v((128, n), F32)
    items["grad1"] = v((128, n), F32)
    items["small"] = v((16, n), F32)
    items["small_buf"] = v((7, 16, 128), F32)
    items["both"] = v((32, 128), F32)
    items["both_buf"] = v((15, 32, 128), F32)
    items["spread"] = v((8, 16, 128), F32)
    items["norms"] = v((2, 8, n), F32)
    items["norms_t"] = v((2, n, 8), F32)
    items["qkv_bias"] = v((2, 1, 384), F32)
    items["in_bias"] = v((2, 1, 512), F32)
    items["out_bias"] = v((2, n), F32)
    items["ss"] = DMA((2, 7))
    items["os"] = DMA((2, 15))
    items["es"] = DMA((2, 7))
    return items


DMA = pltpu.SemaphoreType.DMA


class Refs:
    pass


def whole_kernel(names, *refs):
    z = Refs()
    for name, ref in zip(names, refs):
        setattr(z, name, ref)
    d, t, core, tensor, chips = place()
    other = (d + 1 - 2 * core, t)
    mine_rows = span(t, 128)
    shard = span(d, 64)
    steps = [(r, p) for r in range(4) for p in range(2) if r or p]
    others = [(lax.rem(d + k, 16), t) for k in range(1, 16)]

    for l, w in enumerate((z.w0, z.w1)):
        for c in range(3):
            w[shard, c * 128 : (c + 1) * 128] = z.qkv_w[l, c]
        w[shard, 384:896] = z.in_w[l]
        w[shard, 896:1024] = z.dense_w[l]
        w[shard, 1024:1536] = z.out_w[l]
    z.xg0[mine_rows] = normed(z.tokens[...].astype(F32))[0].astype(BF)
    z.gg1[mine_rows] = z.cotangent[...]

    greet([tensor.device(*s) for s in steps] + others)
    rows0 = Gather(tensor, lambda i: z.xg0.at[span(i, 128)], 128, z.ts0)
    rows0.start()
    weights = {}
    for name, l, columns in (("q", 0, slice(0, 384)), ("f", 0, slice(384, 1536)), ("1", 1, slice(0, 1536))):
        dst = getattr(z, "w%d" % l)
        weights[name] = WeightGather(
            chips, other, core, columns, dst, getattr(z, "ws" + name), getattr(z, "cs" + name)
        )
    weights["q"].start()
    weights["f"].start()
    z.small[...] = jnp.zeros_like(z.small)
    z.both[...] = jnp.zeros_like(z.both)
    z.small[9:10] = jnp.sum(z.cotangent[...].astype(F32), axis=0, keepdims=True)
    for l in range(2):
        norms = jnp.concatenate([z.gain[l].astype(F32), z.shift[l].astype(F32)], axis=0)
        z.norms[l, 0:4] = norms
        z.norms_t[l] = z.norms[l].T
        for c in range(3):
            z.qkv_bias[l, 0:1, c * 128 : (c + 1) * 128] = z.qkv_b[c, l : l + 1].astype(F32)
    for l in range(2):
        z.in_bias[l] = z.in_b[l : l + 1].astype(F32)
    z.out_bias[...] = z.dense_b[...].astype(F32) + z.out_b[...].astype(F32)
    write_tables(z.lengths, z.frequency, z.cosine, z.low, z.high, z.first)
    rows0.middle()
    weights["q"].middle()
    weights["f"].middle()
    rows0.last()
    weights["q"].last()
    weights["f"].last()
    rows0.finish()
    weights["q"].finish()

    def half_gather(h, sems):
        return Gather(tensor, lambda i: z.gg1.at[pl.ds(pl.multiple_of(i * 128 + h * 64, 64), 64)], 64, sems)

    cotangent = [half_gather(0, z.gsa), half_gather(1, z.gsb)]
    cotangent[0].start()

    tables = (z.cosine, z.low, z.high)
    layers = [
        Layer(
            getattr(z, "xg%d" % l), getattr(z, "w%d" % l),
            z.norms.at[l], z.norms_t.at[l],
            z.qkv_bias.at[l], z.in_bias.at[l], tables, z.first,
            [getattr(z, "%s%d" % (name, l)) for name in KEPT],
        )
        for l in range(2)
    ]

    def tensor_scatter(part, buf, sems):
        return Scatter(tensor, lambda i: part.at[span(i, 128)], lambda i: buf.at[i], 128, sems)

    def half_scatter(h, sems):
        rows = slice(h * 64, h * 64 + 64)
        return Scatter(
            tensor, lambda i: z.part_out.at[pl.ds(pl.multiple_of(i * 128 + h * 64, 64), 64)],
            lambda i: z.fbuf1.at[i, rows], 64, sems
        )

    layers[0].project(z.v_t)
    cotangent[0].middle()
    layers[0].attend(z.v_t)
    cotangent[0].last()
    weights["f"].finish()
    weights["1"].start()
    sum0 = tensor_scatter(z.part, z.fbuf0, z.rs0)
    for r in (2, 1, 3, 0):
        layers[0].branch(z.part, lax.rem(tensor.ring + r, 4))
        sum0.go(r)
    sum0.middle()
    weights["1"].middle()
    sum0.last()
    weights["1"].last()
    stream = z.tokens[...].astype(F32) + sum0.finish() + z.out_bias[0:1]
    z.stream1[...] = stream
    z.xg1[mine_rows] = normed(stream)[0].astype(BF)
    rows1 = Gather(tensor, lambda i: z.xg1.at[span(i, 128)], 128, z.ts1)
    rows1.start()
    rows1.middle()
    rows1.last()
    weights["1"].finish()
    cotangent[0].finish()
    rows1.finish()
    cotangent[1].start()

    layers[1].project(z.v_t)
    cotangent[1].middle()
    layers[1].attend(z.v_t)
    cotangent[1].last()
    sum1 = [half_scatter(0, z.rsa), half_scatter(1, z.rsb)]
    for r in (2, 1, 3, 0):
        layers[1].branch(z.part_out, lax.rem(tensor.ring + r, 4))
        sum1[0].go(r)

    def weight_scatter(tag, columns, l, sems, core_sems):
        return WeightScatter(
            chips, other, core, columns, z.dw, z.mine, getattr(z, "core_buf%d" % l),
            getattr(z, "chip_buf%d" % l), sems, core_sems,
        )

    z.dk[...] = jnp.zeros_like(z.dk)
    z.dv[...] = jnp.zeros_like(z.dv)
    cotangent[1].finish()
    layers[1].back_out(z.gg1, z.da, z.da_t)
    layers[1].attend_back((0, 1), z.da, z.da_t, z.dk, z.dv, z.dq_t)
    sum1[0].middle()
    layers[1].attend_back((2, 3), z.da, z.da_t, z.dk, z.dv, z.dq_t)
    sum1[0].last()
    back1 = tensor_scatter(z.part, z.bbuf1, z.bs1)
    for r in (2, 1, 3, 0):
        layers[1].back_in(
            z.part, lax.rem(tensor.ring + r, 4), z.dk, z.dv, z.dq_t, z.proj_grad, z.both, z.small, 23, 4
        )
        back1.go(r)
    layers[1].grads(z.dw, z.gg1, z.proj_grad, "qf")
    weights_back1 = weight_scatter("1", slice(0, 1536), 1, z.ds1, z.dc1)
    weights_back1.start()
    back1.middle()
    weights_back1.spread()
    back1.last()
    grad = stream_back(back1.finish(), z.cotangent[...].astype(F32), z.stream1[...])
    z.grad1[...] = grad
    z.gg0[mine_rows] = grad.astype(BF)
    grads0 = Gather(tensor, lambda i: z.gg0.at[span(i, 128)], 128, z.gs0)
    grads0.start()
    z.small[8:9] = jnp.sum(grad, axis=0, keepdims=True)
    z.dk[...] = jnp.zeros_like(z.dk)
    z.dv[...] = jnp.zeros_like(z.dv)
    grads0.middle()
    weights_back1.middle()
    grads0.last()
    weights_back1.last()
    z.output[0:64] = (z.stream1[0:64] + sum1[0].finish() + z.out_bias[1:2]).astype(BF)
    grads0.finish()
    for r in (2, 1, 3):
        sum1[1].go(r)

    layers[0].back_out(z.gg0, z.da, z.da_t)
    z.dw_out[1] = weights_back1.finish()
    layers[0].grads(z.dw, z.gg0, z.proj_grad, "f")
    weights_back0 = weight_scatter("a", slice(384, 1536), 0, z.dsa, z.dca)
    weights_back0.start()
    layers[0].attend_back((0, 1), z.da, z.da_t, z.dk, z.dv, z.dq_t)
    weights_back0.spread()
    sum1[1].middle()
    layers[0].attend_back((2, 3), z.da, z.da_t, z.dk, z.dv, z.dq_t)
    sum1[1].last()
    back0 = tensor_scatter(z.part, z.bbuf0, z.bs0)
    for r in (2, 1, 3, 0):
        layers[0].back_in(
            z.part, lax.rem(tensor.ring + r, 4), z.dk, z.dv, z.dq_t, z.proj_grad, z.both, z.small, 16, 0
        )
        back0.go(r)
    small = [
        send(z.small.at[:, span(tensor.block(*s), 128)], z.small_buf.at[i], z.ss, i, tensor.device(*s))
        for i, s in enumerate(steps)
    ]
    layers[0].grads(z.dw, z.gg0, z.proj_grad, "q")
    weights_last = weight_scatter("b", slice(0, 384), 0, z.dsb, z.dcb)
    weights_last.start()
    weights_back0.middle()
    back0.middle()
    weights_last.spread()
    weights_back0.last()
    back0.last()
    for c in small:
        c.wait()
    total = z.small[:, span(t, 128)]
    for i in range(7):
        total = total + z.small_buf[i]
    z.both[0:16] = total
    both = [send(z.both, z.both_buf.at[i], z.os, i, p) for i, p in enumerate(others)]
    weights_last.middle()
    weights_last.last()
    for c in both:
        c.wait()
    total = z.both[...]
    for i in range(15):
        total = total + z.both_buf[i]
    z.spread[t] = total[0:16]
    spread = [
        send(z.spread.at[t], z.spread.at[t], z.es, i, tensor.device(*s)) for i, s in enumerate(steps)
    ]
    for l in range(2):
        for c in range(3):
            row = 16 + 7 * l + c
            z.qkv_b_grad[c, l : l + 1] = total[row : row + 1]
        for c in range(4):
            row = 19 + 7 * l + c
            z.in_b_grad[l : l + 1, c * 128 : (c + 1) * 128] = total[row : row + 1]
    z.output[64:128] = (z.stream1[64:128] + sum1[1].finish() + z.out_bias[1:2]).astype(BF)
    z.dw_out[0, :, 384:1536] = weights_back0.finish()
    z.input_grad[...] = stream_back(back0.finish(), z.grad1[...], z.tokens[...].astype(F32))
    z.dw_out[0, :, 0:384] = weights_last.finish()
    for c in spread:
        c.wait()
    for i in range(8):
        lanes = slice(i * 128, (i + 1) * 128)
        for l in range(2):
            z.gain_grad[l, :, lanes] = z.spread[i, 4 * l : 4 * l + 2]
            z.shift_grad[l, :, lanes] = z.spread[i, 4 * l + 2 : 4 * l + 4]
        z.bias_grad[:, lanes] = z.spread[i, 8:10]


def result_kernel(
    output, input_grad, dw, qkv_b_grad, in_b_grad, bias_grad, gain_grad, shift_grad,
    output_to, input_grad_to, qkv_to, qkv_b_to, dense_to, dense_b_to, in_to, in_b_to, out_to, out_b_to,
    gain_to, shift_to,
):
    output_to[...] = output[...]
    input_grad_to[...] = input_grad[...]
    for l in range(2):
        for c in range(3):
            qkv_to[l, c] = dw[l, :, c * 128 : (c + 1) * 128]
        in_to[l] = dw[l, :, 384:896]
        dense_to[l] = dw[l, :, 896:1024]
        out_to[l] = dw[l, :, 1024:1536]
    qkv_b_to[...] = qkv_b_grad[...]
    in_b_to[...] = in_b_grad[...]
    dense_b_to[...] = bias_grad[...]
    out_b_to[...] = bias_grad[...]
    gain_to[...] = gain_grad[...]
    shift_to[...] = shift_grad[...]


def local(
    tokens,
    lengths,
    qkv_weight,
    qkv_bias,
    dense_weight,
    dense_bias,
    fc_in_weight,
    fc_in_bias,
    fc_out_weight,
    fc_out_bias,
    norm_gain,
    norm_bias,
    cotangent,
):
    lane = np.arange(128) % HEAD_DIM
    half_rot = ROT // 2
    frequency = np.where(lane < ROT, 10000.0 ** (-(2.0 * (lane % half_rot)) / ROT), 0.0)
    inputs = (
        tokens,
        cotangent,
        lengths,
        jnp.asarray(frequency[None, :], F32),
        qkv_weight.swapaxes(1, 2),
        fc_in_weight,
        dense_weight.swapaxes(1, 2),
        fc_out_weight.swapaxes(1, 2),
        norm_gain,
        norm_bias,
        qkv_bias.swapaxes(0, 1),
        fc_in_bias,
        dense_bias,
        fc_out_bias,
    )
    s = jax.ShapeDtypeStruct
    shapes = (
        s((128, 1024), BF),
        s((128, 1024), F32),
        s((2, 64, 1536), F32),
        s((3, 2, 128), F32),
        s((2, 512), F32),
        s((2, 1024), F32),
        s((2, 2, 1024), F32),
        s((2, 2, 1024), F32),
    )
    scratch = scratch_list()
    names = INPUTS + OUTPUTS + tuple(scratch)
    results = pl.pallas_call(
        lambda *refs: whole_kernel(names, *refs),
        out_shape=shapes,
        in_specs=[VM] * len(inputs),
        out_specs=(VM,) * len(shapes),
        scratch_shapes=list(scratch.values()),
        compiler_params=pltpu.CompilerParams(
            collective_id=1, has_side_effects=True, vmem_limit_bytes=63 * 2**20
        ),
        cost_estimate=pl.CostEstimate(flops=0, bytes_accessed=600_000_000, transcendentals=0),
        name="layers_forward_and_backward",
    )(*inputs)
    shapes = (
        s((128, 1024), BF),
        s((128, 1024), F32),
        s((2, 3, 64, 128), F32),
        s((3, 2, 128), F32),
        s((2, 64, 128), F32),
        s((2, 1024), F32),
        s((2, 64, 512), F32),
        s((2, 512), F32),
        s((2, 64, 512), F32),
        s((2, 1024), F32),
        s((2, 2, 1024), F32),
        s((2, 2, 1024), F32),
    )
    final = pl.pallas_call(
        result_kernel,
        out_shape=shapes,
        in_specs=[VM] * len(results),
        out_specs=(VM,) * len(shapes),
        compiler_params=pltpu.CompilerParams(vmem_limit_bytes=60 * 2**20),
        cost_estimate=pl.CostEstimate(flops=0, bytes_accessed=6_000_000, transcendentals=0),
        name="results",
    )(*results)
    output, input_grad, qkv, qkv_b, dense, dense_b, fc_in, fc_in_b, fc_out, fc_out_b, gains, shifts = final
    return (
        output,
        input_grad,
        qkv.swapaxes(1, 2),
        qkv_b.swapaxes(0, 1),
        dense.swapaxes(1, 2),
        dense_b,
        fc_in,
        fc_in_b,
        fc_out.swapaxes(1, 2),
        fc_out_b,
        gains,
        shifts,
    )


def solution(mesh):
    return jax.shard_map(
        local,
        mesh=mesh,
        in_specs=(
            P(("dp", "tensor"), None),
            P("dp", None),
            P(None, "dp", None, "tensor"),
            P(None, None, "tensor"),
            P(None, "tensor", "dp"),
            P(),
            P(None, "dp", "tensor"),
            P(None, "tensor"),
            P(None, "tensor", "dp"),
            P(),
            P(),
            P(),
            P(("dp", "tensor"), None),
        ),
        out_specs=(
            P(("dp", "tensor"), None),
            P(("dp", "tensor"), None),
            P(None, "dp", None, "tensor"),
            P(None, None, "tensor"),
            P(None, "tensor", "dp"),
            P(),
            P(None, "dp", "tensor"),
            P(None, "tensor"),
            P(None, "tensor", "dp"),
            P(),
            P(),
            P(),
        ),
        check_vma=False,
    )
```

```python
import jax
import jax.numpy as jnp
import numpy as np
from jax import lax
from jax.experimental import pallas as pl
from jax.experimental.pallas import tpu as pltpu
from jax.sharding import PartitionSpec as P

MESH = pl.DeviceIdType.MESH
HEAD_DIM = 64
ROT = 16
EPSILON = 1e-05
MASKED = -1000000000.0
ROWS = 256
BF = jnp.bfloat16
F32 = jnp.float32
VM = pl.BlockSpec(memory_space=pltpu.VMEM)


class Net:
    def __init__(self, ring, pair, index, device):
        self.ring, self.pair, self.index_of, self.device_of = ring, pair, index, device

    def block(self, r, p):
        return self.index_of(lax.rem(self.ring + r, 4), lax.rem(self.pair + p, 2))

    def device(self, r, p):
        return self.device_of(self.block(r, p))


def place():
    d = lax.axis_index("dp")
    t = lax.axis_index("tensor")
    core = lax.rem(d, 2)
    tensor = Net(t // 2, lax.rem(t, 2), lambda r, p: r * 2 + p, lambda i: (d, i))
    chips = Net(lax.rem(d // 2, 4), d // 8, lambda r, p: p * 4 + r, lambda i: (i * 2 + core, t))
    return d, t, core, tensor, chips


PEERS = [(1, 0), (3, 0), (2, 0), (0, 1)]


def greet(devices):
    barrier = pltpu.get_barrier_semaphore()
    for device in devices:
        pl.semaphore_signal(barrier, inc=1, device_id=device, device_id_type=MESH)
    pl.semaphore_wait(barrier, len(devices))


def send(src, dst, sems, i, device):
    copy = pltpu.make_async_remote_copy(
        src_ref=src,
        dst_ref=dst,
        send_sem=sems.at[0, i],
        recv_sem=sems.at[1, i],
        device_id=device,
        device_id_type=MESH,
    )
    copy.start()
    return copy


class Gather:
    def __init__(self, net, block, rows, sems):
        self.net, self.block, self.rows, self.sems, self.copies = net, block, rows, sems, []

    def at(self, r, p):
        return self.block(self.net.block(r, p))

    def piece(self, r, p, c, n):
        return self.at(r, p).at[pl.ds(c * self.rows // n, self.rows // n)]

    def send(self, block, r, p):
        copy = send(block, block, self.sems, len(self.copies), self.net.device(r, p))
        self.copies.append(copy)
        return copy

    def start(self):
        self.across = self.send(self.at(0, 0), 0, 1)
        self.first = []
        for c in range(2):
            self.first.append((self.send(self.piece(0, 0, c, 4), 1, 0), 1, 3, c))
            self.first.append((self.send(self.piece(0, 0, 2 + c, 4), 3, 0), 3, 1, 2 + c))
        self.up = self.send(self.piece(0, 0, 1, 2), 1, 0)
        self.down = self.send(self.piece(0, 0, 0, 2), 3, 0)

    def middle(self, seen=lambda block: None):
        self.second = []
        for copy, ahead, behind, c in self.first:
            copy.wait_recv()
            self.second.append((self.send(self.piece(behind, 0, c, 4), ahead, 0), c))
        self.across.wait_recv()
        self.up2 = self.send(self.at(0, 1), 1, 0)
        self.down2 = self.send(self.at(0, 1), 3, 0)
        seen(self.at(0, 1))

    def last(self, seen=lambda block: None):
        self.third = []
        for copy, c in self.second:
            copy.wait_recv()
            self.third.append(self.send(self.piece(2, 0, c, 4), 0, 1))
        seen(self.at(2, 0))

    def finish(self, seen=lambda block: None):
        for copies, r, p in (
            ([self.up], 3, 0), ([self.down], 1, 0), ([self.up2], 3, 1), ([self.down2], 1, 1), (self.third, 2, 1)
        ):
            for copy in copies:
                copy.wait_recv()
            seen(self.at(r, p))
        for copy in self.copies:
            copy.wait_send()


def add(ref, *others):
    total = ref[...].astype(F32)
    for other in others:
        total = total + other[...].astype(F32)
    ref[...] = total.astype(BF)


class Scatter:
    def __init__(self, net, part, slot, rows, sems):
        self.net, self.part_of, self.slot, self.rows, self.sems = net, part, slot, rows, sems
        self.copies = []

    def part(self, r, p):
        return self.part_of(self.net.block(r, p))

    def half(self, ref, c):
        return ref.at[pl.ds(c * self.rows // 2, self.rows // 2)]

    def send(self, src, dst, r, p):
        copy = send(src, dst, self.sems, len(self.copies), self.net.device(r, p))
        self.copies.append(copy)
        return copy

    def go(self, r):
        if r == 2:
            self.across = self.send(self.part(2, 1), self.slot(0), 0, 1)
        if r == 1:
            self.up2 = self.send(self.part(1, 1), self.slot(2), 1, 0)
            self.up = self.send(self.half(self.part(1, 0), 0), self.half(self.slot(1), 0), 1, 0)
        if r == 3:
            self.down2 = self.send(self.part(3, 1), self.slot(4), 3, 0)
            self.down = self.send(self.half(self.part(3, 0), 1), self.half(self.slot(3), 1), 3, 0)

    def middle(self):
        self.across.wait_recv()
        add(self.part(2, 0), self.slot(0))
        self.far_down = self.send(self.half(self.part(2, 0), 0), self.half(self.slot(5), 0), 3, 0)
        self.far_up = self.send(self.half(self.part(2, 0), 1), self.half(self.slot(5), 1), 1, 0)
        self.up2.wait_recv()
        self.down2.wait_recv()
        add(self.part(0, 1), self.slot(2), self.slot(4))
        self.across2 = self.send(self.part(0, 1), self.slot(6), 0, 1)

    def last(self):
        self.far_down.wait_recv()
        block = self.half(self.part(3, 0), 0)
        add(block, self.half(self.slot(5), 0))
        self.near_down = self.send(block, self.half(self.slot(3), 0), 3, 0)
        self.far_up.wait_recv()
        block = self.half(self.part(1, 0), 1)
        add(block, self.half(self.slot(5), 1))
        self.near_up = self.send(block, self.half(self.slot(1), 1), 1, 0)

    def finish(self):
        for copy in (self.up, self.down, self.across2, self.near_down, self.near_up):
            copy.wait_recv()
        for copy in self.copies:
            copy.wait_send()
        total = self.part(0, 0)[...].astype(F32)
        for i in (1, 3, 6):
            total = total + self.slot(i)[...].astype(F32)
        return total


class WeightGather:
    def __init__(self, chips, other, core, columns, dst, sems, core_sems):
        block = lambda i: dst.at[span(i * 2 + core, 64), columns]
        self.gather = Gather(chips, block, 64, sems)
        self.other = other
        self.core_sems = core_sems
        self.copies = []

    def pass_on(self, block):
        i = len(self.copies)
        self.copies.append(send(block, block, self.core_sems, i, self.other))

    def start(self):
        self.gather.start()
        self.pass_on(self.gather.at(0, 0))

    def middle(self):
        self.gather.middle(self.pass_on)

    def last(self):
        self.gather.last(self.pass_on)

    def finish(self):
        self.gather.finish(self.pass_on)
        for copy in self.copies:
            copy.wait()


class WeightScatter:
    def __init__(self, chips, other, core, columns, dw, mine, core_buf, buf, sems, core_sems):
        self.core, self.other, self.core_sems, self.columns = core, other, core_sems, columns
        self.dw, self.mine, self.core_buf = dw, mine, core_buf
        slot = lambda ref: lambda i: ref.at[i, :, columns]
        self.scatter = Scatter(chips, slot(mine), slot(buf), 64, sems)

    def start(self):
        c = self.columns
        self.swap = send(
            self.dw.at[:, 1 - self.core, :, c], self.core_buf.at[:, :, c], self.core_sems, 0, self.other
        )

    def spread(self):
        c = self.columns
        self.swap.wait()

        @pl.loop(0, 8)
        def _(i):
            total = self.dw[i, self.core, :, c].astype(F32) + self.core_buf[i, :, c].astype(F32)
            self.mine[i, :, c] = total.astype(BF)

        for r in (2, 1, 3):
            self.scatter.go(r)

    def middle(self):
        self.scatter.middle()

    def last(self):
        self.scatter.last()

    def finish(self):
        return self.scatter.finish()


def normed(x):
    average = jnp.mean(x, axis=-1, keepdims=True)
    centered = x - average
    inv = lax.rsqrt(jnp.mean(centered * centered, axis=-1, keepdims=True) + EPSILON)
    return centered * inv, inv


def stream_back(total, grad, stream):
    xhat, inv = normed(stream)
    first = jnp.mean(total, axis=-1, keepdims=True)
    second = jnp.mean(total * xhat, axis=-1, keepdims=True)
    return grad + inv * (total - first - xhat * second)


def nn(a, b):
    return jnp.dot(a, b, preferred_element_type=F32)


def nt(a, b):
    return lax.dot_general(a, b, (((1,), (1,)), ((), ())), preferred_element_type=F32)


def turned(v, cosine, low, high):
    return v * cosine + pltpu.roll(v, 120, 1) * low + pltpu.roll(v, 8, 1) * high


def head_rows(v, h):
    ids = lax.broadcasted_iota(jnp.int32, v.shape, 0)
    return jnp.where((ids < HEAD_DIM) == (h == 0), v, jnp.zeros_like(v))


def head_lanes(v, h):
    ids = lax.broadcasted_iota(jnp.int32, v.shape, 1)
    return jnp.where((ids < HEAD_DIM) == (h == 0), v, jnp.zeros_like(v))


def allowed(first_ref, i):
    keys = (i + 1) * ROWS
    first = first_ref[:, i * ROWS : (i + 1) * ROWS]
    key = lax.broadcasted_iota(jnp.int32, (keys, ROWS), 0)
    query = lax.broadcasted_iota(jnp.int32, (keys, ROWS), 1) + i * ROWS
    return (key >= first) & (key <= query)


def opening(row, lengths):
    second = lengths[:, 0:1]
    third = second + lengths[:, 1:2]
    return jnp.where(row >= third, third, jnp.where(row >= second, second, 0))


def span(i, size):
    return pl.ds(pl.multiple_of(i * size, size), size)


def write_tables(lengths, frequency, cosine, low, high, first):
    @pl.loop(0, 4)
    def _(i):
        row = lax.broadcasted_iota(jnp.int32, (ROWS, 128), 0) + i * ROWS
        angle = (row - opening(row, lengths[...])).astype(F32) * frequency[...]
        sine = jnp.sin(angle)
        lane = lax.rem(lax.broadcasted_iota(jnp.int32, (ROWS, 128), 1), HEAD_DIM)
        r = span(i, ROWS)
        cosine[r] = jnp.cos(angle)
        low[r] = jnp.where(lane < ROT // 2, -sine, 0.0)
        high[r] = jnp.where(lane < ROT // 2, 0.0, sine)

    first[...] = opening(lax.broadcasted_iota(jnp.int32, first.shape, 1), lengths[...])


KEPT = ("q", "k", "v", "q_t", "k_t", "o_t", "lse", "cat", "slope")


class Layer:
    def __init__(self, xg, w, norms, norms_t, qkv_b, in_b, tables, first, kept):
        self.xg, self.w, self.norms, self.norms_t = xg, w, norms, norms_t
        self.qkv_b, self.in_b = qkv_b, in_b
        self.tables, self.first = tables, first
        for name, ref in zip(KEPT, kept):
            setattr(self, name, ref)

    def project(self, v_t):
        @pl.loop(0, 4)
        def _(i):
            r = span(i, ROWS)
            n1 = (self.xg[r].astype(F32) * self.norms[0:1] + self.norms[2:3]).astype(BF)
            proj = nn(n1, self.w[:, 0:384]) + self.qkv_b[...]
            tables = [table[r] for table in self.tables]
            query = turned(proj[:, 0:128], *tables).astype(BF).astype(F32) * HEAD_DIM**-0.5
            key = turned(proj[:, 128:256], *tables)
            value = proj[:, 256:384]
            for there, flat, across in (
                (query, self.q, self.q_t), (key, self.k, self.k_t), (value, self.v, v_t)
            ):
                flat[r] = there.astype(BF)
                across[:, r] = there.T.astype(BF)

    def attend(self, v_t):
        for i in range(4):
            keys = (i + 1) * ROWS
            r = slice(i * ROWS, keys)
            ok = allowed(self.first, i)
            for h in range(2):
                hs = slice(h * HEAD_DIM, (h + 1) * HEAD_DIM)
                scores = jnp.where(ok, nn(self.k[0:keys], head_rows(self.q_t[:, r], h)), MASKED)
                top = jnp.max(scores, axis=0, keepdims=True)
                weight = jnp.exp(scores - top)
                total = jnp.sum(weight, axis=0, keepdims=True)
                self.o_t[hs, r] = nn(v_t[hs, 0:keys], weight.astype(BF)) / total
                self.lse[h : h + 1, r] = top + jnp.log(total)
            self.cat[r, 0:128] = self.o_t[:, r].T.astype(BF)

    def branch(self, part, block):
        r = span(block, ROWS)
        n2 = (self.xg[r].astype(F32) * self.norms[1:2] + self.norms[3:4]).astype(BF)
        pre = nn(n2, self.w[:, 384:896]) + self.in_b[...]
        bell = 0.5 + 0.5 * lax.erf(pre * 0.5**0.5)
        self.cat[r, 128:640] = (pre * bell).astype(BF)
        self.slope[r] = (bell + pre * jnp.exp(-0.5 * pre * pre) * 0.3989422804014327).astype(BF)
        part[r] = nt(self.cat[r], self.w[:, 896:1536]).astype(BF)

    def back_out(self, gg, da, da_t):
        @pl.loop(0, 4)
        def _(i):
            r = span(i, ROWS)
            cat_grad = nn(gg[r], self.w[:, 896:1536])
            da[r] = cat_grad[:, 0:128].astype(BF)
            da_t[:, r] = cat_grad[:, 0:128].T.astype(BF)
            self.slope[r] = (cat_grad[:, 128:640] * self.slope[r].astype(F32)).astype(BF)

    def attend_back(self, blocks, da, da_t, dk, dv, dq_t):
        for i in blocks:
            keys = (i + 1) * ROWS
            r = slice(i * ROWS, keys)
            ok = allowed(self.first, i)
            for h in range(2):
                hs = slice(h * HEAD_DIM, (h + 1) * HEAD_DIM)
                scores = nn(self.k[0:keys], head_rows(self.q_t[:, r], h))
                prob = jnp.exp(jnp.where(ok, scores, MASKED) - self.lse[h : h + 1, r])
                centre = jnp.sum(da_t[hs, r].astype(F32) * self.o_t[hs, r], axis=0, keepdims=True)
                prob_grad = nn(self.v[0:keys], head_rows(da_t[:, r], h))
                score_grad = (prob * (prob_grad - centre)).astype(BF)
                dv[0:keys] += nn(prob.astype(BF), head_lanes(da[r], h))
                dk[0:keys] += nn(score_grad, head_lanes(self.q[r], h))
                dq_t[hs, r] = nn(self.k_t[hs, 0:keys], score_grad) * HEAD_DIM**-0.5

    def back_in(self, part, block, dk, dv, dq_t, proj_grad, cols, small, where_cols, where_small):
        r = span(block, ROWS)
        tables = self.tables[0][r], -self.tables[1][r], -self.tables[2][r]
        proj_grad[r, 0:128] = turned(dq_t[:, r].T, *tables).astype(BF)
        proj_grad[r, 128:256] = turned(dk[r], *tables).astype(BF)
        proj_grad[r, 256:384] = dv[r].astype(BF)
        pg, hg = proj_grad[r], self.slope[r]
        g1 = nt(pg, self.w[:, 0:384])
        g2 = nt(hg, self.w[:, 384:896])
        part[r] = (g1 * self.norms[0:1] + g2 * self.norms[1:2]).astype(BF)
        for grad, n, at in ((pg, 3, 0), (hg, 4, 3)):
            sums = jnp.sum(grad.astype(F32), axis=0, keepdims=True)
            for c in range(n):
                row = where_cols + at + c
                cols[row : row + 1] += sums[:, c * 128 : (c + 1) * 128]
        x = self.xg[r].astype(F32)
        for j, sums in enumerate((g1 * x, g2 * x, g1, g2)):
            row = where_small + j
            small[row : row + 1] += jnp.sum(sums, axis=0, keepdims=True)

    def grads(self, dw, gg, proj_grad, which):
        @pl.loop(0, 4)
        def _(j):
            c = span(j, ROWS)
            chips = pl.ds(j * 2, 2)

            def put(left, right, columns):
                dw[chips, :, :, columns] = nn(left, right).astype(BF).reshape(2, 2, 64, right.shape[1])

            x_t = self.xg[:, c].T.astype(F32)
            if "q" in which:
                n1_t = (x_t * self.norms_t[c, 0:1] + self.norms_t[c, 2:3]).astype(BF)
                put(n1_t, proj_grad[...], slice(0, 384))
            if "f" in which:
                n2_t = (x_t * self.norms_t[c, 1:2] + self.norms_t[c, 3:4]).astype(BF)
                put(n2_t, self.slope[...], slice(384, 896))
                put(gg[:, c].T, self.cat[...], slice(896, 1536))


INPUTS = (
    "tokens", "cotangent", "lengths", "frequency", "qkv_w", "in_w", "dense_w", "out_w",
    "gain", "shift", "qkv_b", "in_b", "dense_b", "out_b",
)
OUTPUTS = ("output", "input_grad", "dw_out", "qkv_b_grad", "in_b_grad", "bias_grad", "gain_grad", "shift_grad")


def scratch_list():
    n = 1024
    v = pltpu.VMEM
    items = {}
    for l in "01":
        items["xg" + l] = v((n, n), BF)
        items["gg" + l] = v((n, n), BF)
        items["w" + l] = v((n, 1536), BF)
        items["core_buf" + l] = v((8, 64, 1536), BF)
        items["chip_buf" + l] = v((7, 64, 1536), BF)
        for name in ("q", "k", "v"):
            items[name + l] = v((n, 128), BF)
        for name in ("q_t", "k_t"):
            items[name + l] = v((128, n), BF)
        items["o_t" + l] = v((128, n), F32)
        items["lse" + l] = v((8, n), F32)
        items["cat" + l] = v((n, 640), BF)
        items["slope" + l] = v((n, 512), BF)
        items["bs" + l] = DMA((2, 10))
        items["ts" + l] = DMA((2, 17))
        for name in ("fbuf", "bbuf"):
            items[name + l] = v((7, 128, n), BF)
    for l in ("q", "f", "1"):
        items["ws" + l] = DMA((2, 17))
        items["cs" + l] = DMA((2, 8))
    for l in "0ab":
        items["rs" + l] = DMA((2, 10))
        items["gs" + l] = DMA((2, 17))
    for l in ("1", "a", "b"):
        items["ds" + l] = DMA((2, 10))
        items["dc" + l] = DMA((2, 1))
    items["v_t"] = v((128, n), BF)
    items["part"] = v((n, n), BF)
    items["part_out"] = v((n, n), BF)
    items["dw"] = v((8, 2, 64, 1536), BF)
    items["mine"] = v((8, 64, 1536), BF)
    for name in ("cosine", "low", "high"):
        items[name] = v((n, 128), F32)
    items["first"] = v((1, n), jnp.int32)
    items["da"] = v((n, 128), BF)
    items["da_t"] = v((128, n), BF)
    items["proj_grad"] = v((n, 384), BF)
    items["dk"] = v((n, 128), F32)
    items["dv"] = v((n, 128), F32)
    items["dq_t"] = v((128, n), F32)
    items["stream1"] = v((128, n), F32)
    items["grad1"] = v((128, n), F32)
    items["small"] = v((16, n), F32)
    items["small_buf"] = v((7, 16, 128), F32)
    items["both"] = v((32, 128), F32)
    items["both_buf"] = v((15, 32, 128), F32)
    items["spread"] = v((8, 16, 128), F32)
    items["norms"] = v((2, 8, n), F32)
    items["norms_t"] = v((2, n, 8), F32)
    items["qkv_bias"] = v((2, 1, 384), F32)
    items["in_bias"] = v((2, 1, 512), F32)
    items["out_bias"] = v((2, n), F32)
    items["ss"] = DMA((2, 7))
    items["os"] = DMA((2, 15))
    items["es"] = DMA((2, 7))
    return items


DMA = pltpu.SemaphoreType.DMA


class Refs:
    pass


def whole_kernel(names, *refs):
    z = Refs()
    for name, ref in zip(names, refs):
        setattr(z, name, ref)
    d, t, core, tensor, chips = place()
    other = (d + 1 - 2 * core, t)
    mine_rows = span(t, 128)
    shard = span(d, 64)
    steps = [(r, p) for r in range(4) for p in range(2) if r or p]
    others = [(lax.rem(d + k, 16), t) for k in range(1, 16)]

    for l, w in enumerate((z.w0, z.w1)):
        for c in range(3):
            w[shard, c * 128 : (c + 1) * 128] = z.qkv_w[l, c]
        w[shard, 384:896] = z.in_w[l]
        w[shard, 896:1024] = z.dense_w[l]
        w[shard, 1024:1536] = z.out_w[l]
    z.xg0[mine_rows] = normed(z.tokens[...].astype(F32))[0].astype(BF)
    z.gg1[mine_rows] = z.cotangent[...]

    greet([tensor.device(*s) for s in steps] + others)
    rows0 = Gather(tensor, lambda i: z.xg0.at[span(i, 128)], 128, z.ts0)
    rows0.start()
    weights = {}
    for name, l, columns in (("q", 0, slice(0, 384)), ("f", 0, slice(384, 1536)), ("1", 1, slice(0, 1536))):
        dst = getattr(z, "w%d" % l)
        weights[name] = WeightGather(
            chips, other, core, columns, dst, getattr(z, "ws" + name), getattr(z, "cs" + name)
        )
    weights["q"].start()
    weights["f"].start()
    z.small[...] = jnp.zeros_like(z.small)
    z.both[...] = jnp.zeros_like(z.both)
    z.small[9:10] = jnp.sum(z.cotangent[...].astype(F32), axis=0, keepdims=True)
    for l in range(2):
        norms = jnp.concatenate([z.gain[l].astype(F32), z.shift[l].astype(F32)], axis=0)
        z.norms[l, 0:4] = norms
        z.norms_t[l] = z.norms[l].T
        for c in range(3):
            z.qkv_bias[l, 0:1, c * 128 : (c + 1) * 128] = z.qkv_b[c, l : l + 1].astype(F32)
    for l in range(2):
        z.in_bias[l] = z.in_b[l : l + 1].astype(F32)
    z.out_bias[...] = z.dense_b[...].astype(F32) + z.out_b[...].astype(F32)
    write_tables(z.lengths, z.frequency, z.cosine, z.low, z.high, z.first)
    rows0.middle()
    weights["q"].middle()
    weights["f"].middle()
    rows0.last()
    weights["q"].last()
    weights["f"].last()
    rows0.finish()
    weights["q"].finish()

    def half_gather(h, sems):
        return Gather(tensor, lambda i: z.gg1.at[pl.ds(pl.multiple_of(i * 128 + h * 64, 64), 64)], 64, sems)

    cotangent = [half_gather(0, z.gsa), half_gather(1, z.gsb)]
    cotangent[0].start()

    tables = (z.cosine, z.low, z.high)
    layers = [
        Layer(
            getattr(z, "xg%d" % l), getattr(z, "w%d" % l),
            z.norms.at[l], z.norms_t.at[l],
            z.qkv_bias.at[l], z.in_bias.at[l], tables, z.first,
            [getattr(z, "%s%d" % (name, l)) for name in KEPT],
        )
        for l in range(2)
    ]

    def tensor_scatter(part, buf, sems):
        return Scatter(tensor, lambda i: part.at[span(i, 128)], lambda i: buf.at[i], 128, sems)

    def half_scatter(h, sems):
        rows = slice(h * 64, h * 64 + 64)
        return Scatter(
            tensor, lambda i: z.part_out.at[pl.ds(pl.multiple_of(i * 128 + h * 64, 64), 64)],
            lambda i: z.fbuf1.at[i, rows], 64, sems
        )

    layers[0].project(z.v_t)
    cotangent[0].middle()
    layers[0].attend(z.v_t)
    cotangent[0].last()
    weights["f"].finish()
    weights["1"].start()
    sum0 = tensor_scatter(z.part, z.fbuf0, z.rs0)
    for r in (2, 1, 3, 0):
        layers[0].branch(z.part, lax.rem(tensor.ring + r, 4))
        sum0.go(r)
    sum0.middle()
    sum0.last()
    weights["1"].middle()
    stream = z.tokens[...].astype(F32) + sum0.finish() + z.out_bias[0:1]
    z.stream1[...] = stream
    z.xg1[mine_rows] = normed(stream)[0].astype(BF)
    rows1 = Gather(tensor, lambda i: z.xg1.at[span(i, 128)], 128, z.ts1)
    rows1.start()
    weights["1"].last()
    rows1.middle()
    rows1.last()
    weights["1"].finish()
    cotangent[0].finish()
    rows1.finish()
    cotangent[1].start()

    layers[1].project(z.v_t)
    cotangent[1].middle()
    layers[1].attend(z.v_t)
    cotangent[1].last()
    sum1 = [half_scatter(0, z.rsa), half_scatter(1, z.rsb)]
    for r in (2, 1, 3, 0):
        layers[1].branch(z.part_out, lax.rem(tensor.ring + r, 4))
        sum1[0].go(r)

    def weight_scatter(tag, columns, l, sems, core_sems):
        return WeightScatter(
            chips, other, core, columns, z.dw, z.mine, getattr(z, "core_buf%d" % l),
            getattr(z, "chip_buf%d" % l), sems, core_sems,
        )

    z.dk[...] = jnp.zeros_like(z.dk)
    z.dv[...] = jnp.zeros_like(z.dv)
    cotangent[1].finish()
    layers[1].back_out(z.gg1, z.da, z.da_t)
    layers[1].attend_back((0, 1), z.da, z.da_t, z.dk, z.dv, z.dq_t)
    sum1[0].middle()
    layers[1].attend_back((2, 3), z.da, z.da_t, z.dk, z.dv, z.dq_t)
    sum1[0].last()
    back1 = tensor_scatter(z.part, z.bbuf1, z.bs1)
    for r in (2, 1, 3, 0):
        layers[1].back_in(
            z.part, lax.rem(tensor.ring + r, 4), z.dk, z.dv, z.dq_t, z.proj_grad, z.both, z.small, 23, 4
        )
        back1.go(r)
    layers[1].grads(z.dw, z.gg1, z.proj_grad, "f")
    back1.middle()
    layers[1].grads(z.dw, z.gg1, z.proj_grad, "q")
    weights_back1 = weight_scatter("1", slice(0, 1536), 1, z.ds1, z.dc1)
    weights_back1.start()
    back1.last()
    grad = stream_back(back1.finish(), z.cotangent[...].astype(F32), z.stream1[...])
    z.grad1[...] = grad
    z.gg0[mine_rows] = grad.astype(BF)
    grads0 = Gather(tensor, lambda i: z.gg0.at[span(i, 128)], 128, z.gs0)
    grads0.start()
    weights_back1.spread()
    z.small[8:9] = jnp.sum(grad, axis=0, keepdims=True)
    z.dk[...] = jnp.zeros_like(z.dk)
    z.dv[...] = jnp.zeros_like(z.dv)
    grads0.middle()
    grads0.last()
    weights_back1.middle()
    z.output[0:64] = (z.stream1[0:64] + sum1[0].finish() + z.out_bias[1:2]).astype(BF)
    grads0.finish()
    for r in (2, 1, 3):
        sum1[1].go(r)

    layers[0].back_out(z.gg0, z.da, z.da_t)
    weights_back1.last()
    layers[0].grads(z.dw, z.gg0, z.proj_grad, "f")
    weights_back0 = weight_scatter("a", slice(384, 1536), 0, z.dsa, z.dca)
    weights_back0.start()
    layers[0].attend_back((0, 1), z.da, z.da_t, z.dk, z.dv, z.dq_t)
    z.dw_out[1] = weights_back1.finish()
    weights_back0.spread()
    sum1[1].middle()
    layers[0].attend_back((2, 3), z.da, z.da_t, z.dk, z.dv, z.dq_t)
    sum1[1].last()
    back0 = tensor_scatter(z.part, z.bbuf0, z.bs0)
    for r in (2, 1, 3, 0):
        layers[0].back_in(
            z.part, lax.rem(tensor.ring + r, 4), z.dk, z.dv, z.dq_t, z.proj_grad, z.both, z.small, 16, 0
        )
        back0.go(r)
    small = [
        send(z.small.at[:, span(tensor.block(*s), 128)], z.small_buf.at[i], z.ss, i, tensor.device(*s))
        for i, s in enumerate(steps)
    ]
    layers[0].grads(z.dw, z.gg0, z.proj_grad, "q")
    weights_last = weight_scatter("b", slice(0, 384), 0, z.dsb, z.dcb)
    weights_last.start()
    weights_back0.middle()
    back0.middle()
    weights_last.spread()
    weights_back0.last()
    back0.last()
    for c in small:
        c.wait()
    total = z.small[:, span(t, 128)]
    for i in range(7):
        total = total + z.small_buf[i]
    z.both[0:16] = total
    both = [send(z.both, z.both_buf.at[i], z.os, i, p) for i, p in enumerate(others)]
    weights_last.middle()
    weights_last.last()
    for c in both:
        c.wait()
    total = z.both[...]
    for i in range(15):
        total = total + z.both_buf[i]
    z.spread[t] = total[0:16]
    spread = [
        send(z.spread.at[t], z.spread.at[t], z.es, i, tensor.device(*s)) for i, s in enumerate(steps)
    ]
    for l in range(2):
        for c in range(3):
            row = 16 + 7 * l + c
            z.qkv_b_grad[c, l : l + 1] = total[row : row + 1]
        for c in range(4):
            row = 19 + 7 * l + c
            z.in_b_grad[l : l + 1, c * 128 : (c + 1) * 128] = total[row : row + 1]
    z.output[64:128] = (z.stream1[64:128] + sum1[1].finish() + z.out_bias[1:2]).astype(BF)
    z.dw_out[0, :, 384:1536] = weights_back0.finish()
    z.input_grad[...] = stream_back(back0.finish(), z.grad1[...], z.tokens[...].astype(F32))
    z.dw_out[0, :, 0:384] = weights_last.finish()
    for c in spread:
        c.wait()
    for i in range(8):
        lanes = slice(i * 128, (i + 1) * 128)
        for l in range(2):
            z.gain_grad[l, :, lanes] = z.spread[i, 4 * l : 4 * l + 2]
            z.shift_grad[l, :, lanes] = z.spread[i, 4 * l + 2 : 4 * l + 4]
        z.bias_grad[:, lanes] = z.spread[i, 8:10]


def result_kernel(
    output, input_grad, dw, qkv_b_grad, in_b_grad, bias_grad, gain_grad, shift_grad,
    output_to, input_grad_to, qkv_to, qkv_b_to, dense_to, dense_b_to, in_to, in_b_to, out_to, out_b_to,
    gain_to, shift_to,
):
    output_to[...] = output[...]
    input_grad_to[...] = input_grad[...]
    for l in range(2):
        for c in range(3):
            qkv_to[l, c] = dw[l, :, c * 128 : (c + 1) * 128]
        in_to[l] = dw[l, :, 384:896]
        dense_to[l] = dw[l, :, 896:1024]
        out_to[l] = dw[l, :, 1024:1536]
    qkv_b_to[...] = qkv_b_grad[...]
    in_b_to[...] = in_b_grad[...]
    dense_b_to[...] = bias_grad[...]
    out_b_to[...] = bias_grad[...]
    gain_to[...] = gain_grad[...]
    shift_to[...] = shift_grad[...]


def local(
    tokens,
    lengths,
    qkv_weight,
    qkv_bias,
    dense_weight,
    dense_bias,
    fc_in_weight,
    fc_in_bias,
    fc_out_weight,
    fc_out_bias,
    norm_gain,
    norm_bias,
    cotangent,
):
    lane = np.arange(128) % HEAD_DIM
    half_rot = ROT // 2
    frequency = np.where(lane < ROT, 10000.0 ** (-(2.0 * (lane % half_rot)) / ROT), 0.0)
    inputs = (
        tokens,
        cotangent,
        lengths,
        jnp.asarray(frequency[None, :], F32),
        qkv_weight.swapaxes(1, 2),
        fc_in_weight,
        dense_weight.swapaxes(1, 2),
        fc_out_weight.swapaxes(1, 2),
        norm_gain,
        norm_bias,
        qkv_bias.swapaxes(0, 1),
        fc_in_bias,
        dense_bias,
        fc_out_bias,
    )
    s = jax.ShapeDtypeStruct
    shapes = (
        s((128, 1024), BF),
        s((128, 1024), F32),
        s((2, 64, 1536), F32),
        s((3, 2, 128), F32),
        s((2, 512), F32),
        s((2, 1024), F32),
        s((2, 2, 1024), F32),
        s((2, 2, 1024), F32),
    )
    scratch = scratch_list()
    names = INPUTS + OUTPUTS + tuple(scratch)
    results = pl.pallas_call(
        lambda *refs: whole_kernel(names, *refs),
        out_shape=shapes,
        in_specs=[VM] * len(inputs),
        out_specs=(VM,) * len(shapes),
        scratch_shapes=list(scratch.values()),
        compiler_params=pltpu.CompilerParams(
            collective_id=1, has_side_effects=True, vmem_limit_bytes=63 * 2**20
        ),
        cost_estimate=pl.CostEstimate(flops=0, bytes_accessed=600_000_000, transcendentals=0),
        name="layers_forward_and_backward",
    )(*inputs)
    shapes = (
        s((128, 1024), BF),
        s((128, 1024), F32),
        s((2, 3, 64, 128), F32),
        s((3, 2, 128), F32),
        s((2, 64, 128), F32),
        s((2, 1024), F32),
        s((2, 64, 512), F32),
        s((2, 512), F32),
        s((2, 64, 512), F32),
        s((2, 1024), F32),
        s((2, 2, 1024), F32),
        s((2, 2, 1024), F32),
    )
    final = pl.pallas_call(
        result_kernel,
        out_shape=shapes,
        in_specs=[VM] * len(results),
        out_specs=(VM,) * len(shapes),
        compiler_params=pltpu.CompilerParams(vmem_limit_bytes=60 * 2**20),
        cost_estimate=pl.CostEstimate(flops=0, bytes_accessed=6_000_000, transcendentals=0),
        name="results",
    )(*results)
    output, input_grad, qkv, qkv_b, dense, dense_b, fc_in, fc_in_b, fc_out, fc_out_b, gains, shifts = final
    return (
        output,
        input_grad,
        qkv.swapaxes(1, 2),
        qkv_b.swapaxes(0, 1),
        dense.swapaxes(1, 2),
        dense_b,
        fc_in,
        fc_in_b,
        fc_out.swapaxes(1, 2),
        fc_out_b,
        gains,
        shifts,
    )


def solution(mesh):
    return jax.shard_map(
        local,
        mesh=mesh,
        in_specs=(
            P(("dp", "tensor"), None),
            P("dp", None),
            P(None, "dp", None, "tensor"),
            P(None, None, "tensor"),
            P(None, "tensor", "dp"),
            P(),
            P(None, "dp", "tensor"),
            P(None, "tensor"),
            P(None, "tensor", "dp"),
            P(),
            P(),
            P(),
            P(("dp", "tensor"), None),
        ),
        out_specs=(
            P(("dp", "tensor"), None),
            P(("dp", "tensor"), None),
            P(None, "dp", None, "tensor"),
            P(None, None, "tensor"),
            P(None, "tensor", "dp"),
            P(),
            P(None, "dp", "tensor"),
            P(None, "tensor"),
            P(None, "tensor", "dp"),
            P(),
            P(),
            P(),
        ),
        check_vma=False,
    )
```

```python
import jax
import jax.numpy as jnp
import numpy as np
from jax import lax
from jax.experimental import pallas as pl
from jax.experimental.pallas import tpu as pltpu
from jax.sharding import PartitionSpec as P

MESH = pl.DeviceIdType.MESH
HEAD_DIM = 64
ROT = 16
EPSILON = 1e-05
MASKED = -1000000000.0
ROWS = 256
BF = jnp.bfloat16
F32 = jnp.float32
VM = pl.BlockSpec(memory_space=pltpu.VMEM)


class Net:
    def __init__(self, ring, pair, index, device):
        self.ring, self.pair, self.index_of, self.device_of = ring, pair, index, device

    def block(self, r, p):
        return self.index_of(lax.rem(self.ring + r, 4), lax.rem(self.pair + p, 2))

    def device(self, r, p):
        return self.device_of(self.block(r, p))


def place():
    d = lax.axis_index("dp")
    t = lax.axis_index("tensor")
    core = lax.rem(d, 2)
    tensor = Net(t // 2, lax.rem(t, 2), lambda r, p: r * 2 + p, lambda i: (d, i))
    chips = Net(lax.rem(d // 2, 4), d // 8, lambda r, p: p * 4 + r, lambda i: (i * 2 + core, t))
    return d, t, core, tensor, chips


PEERS = [(1, 0), (3, 0), (2, 0), (0, 1)]


def greet(devices):
    barrier = pltpu.get_barrier_semaphore()
    for device in devices:
        pl.semaphore_signal(barrier, inc=1, device_id=device, device_id_type=MESH)
    pl.semaphore_wait(barrier, len(devices))


def send(src, dst, sems, i, device):
    copy = pltpu.make_async_remote_copy(
        src_ref=src,
        dst_ref=dst,
        send_sem=sems.at[0, i],
        recv_sem=sems.at[1, i],
        device_id=device,
        device_id_type=MESH,
    )
    copy.start()
    return copy


class Gather:
    def __init__(self, net, block, rows, sems):
        self.net, self.block, self.rows, self.sems, self.copies = net, block, rows, sems, []

    def at(self, r, p):
        return self.block(self.net.block(r, p))

    def piece(self, r, p, c, n):
        return self.at(r, p).at[pl.ds(c * self.rows // n, self.rows // n)]

    def send(self, block, r, p):
        copy = send(block, block, self.sems, len(self.copies), self.net.device(r, p))
        self.copies.append(copy)
        return copy

    def start(self):
        self.across = self.send(self.at(0, 0), 0, 1)
        self.first = []
        for c in range(2):
            self.first.append((self.send(self.piece(0, 0, c, 4), 1, 0), 1, 3, c))
            self.first.append((self.send(self.piece(0, 0, 2 + c, 4), 3, 0), 3, 1, 2 + c))
        self.up = self.send(self.piece(0, 0, 1, 2), 1, 0)
        self.down = self.send(self.piece(0, 0, 0, 2), 3, 0)

    def middle(self, seen=lambda block: None):
        self.second = []
        for copy, ahead, behind, c in self.first:
            copy.wait_recv()
            self.second.append((self.send(self.piece(behind, 0, c, 4), ahead, 0), c))
        self.across.wait_recv()
        self.up2 = self.send(self.at(0, 1), 1, 0)
        self.down2 = self.send(self.at(0, 1), 3, 0)
        seen(self.at(0, 1))

    def last(self, seen=lambda block: None):
        self.third = []
        for copy, c in self.second:
            copy.wait_recv()
            self.third.append(self.send(self.piece(2, 0, c, 4), 0, 1))
        seen(self.at(2, 0))

    def near(self, seen=lambda block: None):
        for copy, r, p in (
            (self.up, 3, 0), (self.down, 1, 0), (self.up2, 3, 1), (self.down2, 1, 1)
        ):
            copy.wait_recv()
            seen(self.at(r, p))

    def far(self, seen=lambda block: None):
        for copy in self.third:
            copy.wait_recv()
        seen(self.at(2, 1))
        for copy in self.copies:
            copy.wait_send()

    def finish(self, seen=lambda block: None):
        self.near(seen)
        self.far(seen)


def add(ref, *others):
    total = ref[...].astype(F32)
    for other in others:
        total = total + other[...].astype(F32)
    ref[...] = total.astype(BF)


class Scatter:
    def __init__(self, net, part, slot, rows, sems):
        self.net, self.part_of, self.slot, self.rows, self.sems = net, part, slot, rows, sems
        self.copies = []

    def part(self, r, p):
        return self.part_of(self.net.block(r, p))

    def half(self, ref, c):
        return ref.at[pl.ds(c * self.rows // 2, self.rows // 2)]

    def send(self, src, dst, r, p):
        copy = send(src, dst, self.sems, len(self.copies), self.net.device(r, p))
        self.copies.append(copy)
        return copy

    def go(self, r):
        if r == 2:
            self.across = self.send(self.part(2, 1), self.slot(0), 0, 1)
        if r == 1:
            self.up2 = self.send(self.part(1, 1), self.slot(2), 1, 0)
            self.up = self.send(self.half(self.part(1, 0), 0), self.half(self.slot(1), 0), 1, 0)
        if r == 3:
            self.down2 = self.send(self.part(3, 1), self.slot(4), 3, 0)
            self.down = self.send(self.half(self.part(3, 0), 1), self.half(self.slot(3), 1), 3, 0)

    def middle(self):
        self.across.wait_recv()
        add(self.part(2, 0), self.slot(0))
        self.far_down = self.send(self.half(self.part(2, 0), 0), self.half(self.slot(5), 0), 3, 0)
        self.far_up = self.send(self.half(self.part(2, 0), 1), self.half(self.slot(5), 1), 1, 0)
        self.up2.wait_recv()
        self.down2.wait_recv()
        add(self.part(0, 1), self.slot(2), self.slot(4))
        self.across2 = self.send(self.part(0, 1), self.slot(6), 0, 1)

    def last(self):
        self.far_down.wait_recv()
        block = self.half(self.part(3, 0), 0)
        add(block, self.half(self.slot(5), 0))
        self.near_down = self.send(block, self.half(self.slot(3), 0), 3, 0)
        self.far_up.wait_recv()
        block = self.half(self.part(1, 0), 1)
        add(block, self.half(self.slot(5), 1))
        self.near_up = self.send(block, self.half(self.slot(1), 1), 1, 0)

    def finish(self):
        for copy in (self.up, self.down, self.across2, self.near_down, self.near_up):
            copy.wait_recv()
        for copy in self.copies:
            copy.wait_send()
        total = self.part(0, 0)[...].astype(F32)
        for i in (1, 3, 6):
            total = total + self.slot(i)[...].astype(F32)
        return total


class WeightGather:
    def __init__(self, chips, other, core, columns, dst, sems, core_sems):
        block = lambda i: dst.at[span(i * 2 + core, 64), columns]
        self.gather = Gather(chips, block, 64, sems)
        self.other = other
        self.core_sems = core_sems
        self.copies = []

    def pass_on(self, block):
        i = len(self.copies)
        self.copies.append(send(block, block, self.core_sems, i, self.other))

    def start(self):
        self.gather.start()
        self.pass_on(self.gather.at(0, 0))

    def middle(self):
        self.gather.middle(self.pass_on)

    def last(self):
        self.gather.last(self.pass_on)

    def finish(self):
        self.gather.finish(self.pass_on)
        for copy in self.copies:
            copy.wait()


class WeightScatter:
    def __init__(self, chips, other, core, columns, dw, mine, core_buf, buf, sems, core_sems):
        self.core, self.other, self.core_sems, self.columns = core, other, core_sems, columns
        self.dw, self.mine, self.core_buf = dw, mine, core_buf
        slot = lambda ref: lambda i: ref.at[i, :, columns]
        self.scatter = Scatter(chips, slot(mine), slot(buf), 64, sems)

    def start(self):
        c = self.columns
        self.swap = send(
            self.dw.at[:, 1 - self.core, :, c], self.core_buf.at[:, :, c], self.core_sems, 0, self.other
        )

    def spread(self):
        c = self.columns
        self.swap.wait()

        @pl.loop(0, 8)
        def _(i):
            total = self.dw[i, self.core, :, c].astype(F32) + self.core_buf[i, :, c].astype(F32)
            self.mine[i, :, c] = total.astype(BF)

        for r in (2, 1, 3):
            self.scatter.go(r)

    def middle(self):
        self.scatter.middle()

    def last(self):
        self.scatter.last()

    def finish(self):
        return self.scatter.finish()


def normed(x):
    average = jnp.mean(x, axis=-1, keepdims=True)
    centered = x - average
    inv = lax.rsqrt(jnp.mean(centered * centered, axis=-1, keepdims=True) + EPSILON)
    return centered * inv, inv


def stream_back(total, grad, stream):
    xhat, inv = normed(stream)
    first = jnp.mean(total, axis=-1, keepdims=True)
    second = jnp.mean(total * xhat, axis=-1, keepdims=True)
    return grad + inv * (total - first - xhat * second)


def nn(a, b):
    return jnp.dot(a, b, preferred_element_type=F32)


def nt(a, b):
    return lax.dot_general(a, b, (((1,), (1,)), ((), ())), preferred_element_type=F32)


def turned(v, cosine, low, high):
    return v * cosine + pltpu.roll(v, 120, 1) * low + pltpu.roll(v, 8, 1) * high


def head_rows(v, h):
    ids = lax.broadcasted_iota(jnp.int32, v.shape, 0)
    return jnp.where((ids < HEAD_DIM) == (h == 0), v, jnp.zeros_like(v))


def head_lanes(v, h):
    ids = lax.broadcasted_iota(jnp.int32, v.shape, 1)
    return jnp.where((ids < HEAD_DIM) == (h == 0), v, jnp.zeros_like(v))


def allowed(first_ref, i):
    keys = (i + 1) * ROWS
    first = first_ref[:, i * ROWS : (i + 1) * ROWS]
    key = lax.broadcasted_iota(jnp.int32, (keys, ROWS), 0)
    query = lax.broadcasted_iota(jnp.int32, (keys, ROWS), 1) + i * ROWS
    return (key >= first) & (key <= query)


def opening(row, lengths):
    second = lengths[:, 0:1]
    third = second + lengths[:, 1:2]
    return jnp.where(row >= third, third, jnp.where(row >= second, second, 0))


def span(i, size):
    return pl.ds(pl.multiple_of(i * size, size), size)


def write_tables(lengths, frequency, cosine, low, high, first):
    @pl.loop(0, 4)
    def _(i):
        row = lax.broadcasted_iota(jnp.int32, (ROWS, 128), 0) + i * ROWS
        angle = (row - opening(row, lengths[...])).astype(F32) * frequency[...]
        sine = jnp.sin(angle)
        lane = lax.rem(lax.broadcasted_iota(jnp.int32, (ROWS, 128), 1), HEAD_DIM)
        r = span(i, ROWS)
        cosine[r] = jnp.cos(angle)
        low[r] = jnp.where(lane < ROT // 2, -sine, 0.0)
        high[r] = jnp.where(lane < ROT // 2, 0.0, sine)

    first[...] = opening(lax.broadcasted_iota(jnp.int32, first.shape, 1), lengths[...])


KEPT = ("q", "k", "v", "q_t", "k_t", "o_t", "lse", "cat", "slope")


class Layer:
    def __init__(self, xg, w, norms, norms_t, qkv_b, in_b, tables, first, kept):
        self.xg, self.w, self.norms, self.norms_t = xg, w, norms, norms_t
        self.qkv_b, self.in_b = qkv_b, in_b
        self.tables, self.first = tables, first
        for name, ref in zip(KEPT, kept):
            setattr(self, name, ref)

    def project(self, v_t, blocks):
        for block in blocks:
            r = span(block, ROWS)
            n1 = (self.xg[r].astype(F32) * self.norms[0:1] + self.norms[2:3]).astype(BF)
            proj = nn(n1, self.w[:, 0:384]) + self.qkv_b[...]
            tables = [table[r] for table in self.tables]
            query = turned(proj[:, 0:128], *tables).astype(BF).astype(F32) * HEAD_DIM**-0.5
            key = turned(proj[:, 128:256], *tables)
            value = proj[:, 256:384]
            for there, flat, across in (
                (query, self.q, self.q_t), (key, self.k, self.k_t), (value, self.v, v_t)
            ):
                flat[r] = there.astype(BF)
                across[:, r] = there.T.astype(BF)

    def attend(self, v_t):
        for i in range(4):
            keys = (i + 1) * ROWS
            r = slice(i * ROWS, keys)
            ok = allowed(self.first, i)
            for h in range(2):
                hs = slice(h * HEAD_DIM, (h + 1) * HEAD_DIM)
                scores = jnp.where(ok, nn(self.k[0:keys], head_rows(self.q_t[:, r], h)), MASKED)
                top = jnp.max(scores, axis=0, keepdims=True)
                weight = jnp.exp(scores - top)
                total = jnp.sum(weight, axis=0, keepdims=True)
                self.o_t[hs, r] = nn(v_t[hs, 0:keys], weight.astype(BF)) / total
                self.lse[h : h + 1, r] = top + jnp.log(total)
            self.cat[r, 0:128] = self.o_t[:, r].T.astype(BF)

    def branch(self, part, block):
        r = span(block, ROWS)
        n2 = (self.xg[r].astype(F32) * self.norms[1:2] + self.norms[3:4]).astype(BF)
        pre = nn(n2, self.w[:, 384:896]) + self.in_b[...]
        bell = 0.5 + 0.5 * lax.erf(pre * 0.5**0.5)
        self.cat[r, 128:640] = (pre * bell).astype(BF)
        self.slope[r] = (bell + pre * jnp.exp(-0.5 * pre * pre) * 0.3989422804014327).astype(BF)
        part[r] = nt(self.cat[r], self.w[:, 896:1536]).astype(BF)

    def back_out(self, gg, da, da_t, blocks):
        for block in blocks:
            r = span(block, ROWS)
            cat_grad = nn(gg[r], self.w[:, 896:1536])
            da[r] = cat_grad[:, 0:128].astype(BF)
            da_t[:, r] = cat_grad[:, 0:128].T.astype(BF)
            self.slope[r] = (cat_grad[:, 128:640] * self.slope[r].astype(F32)).astype(BF)

    def attend_back(self, blocks, da, da_t, dk, dv, dq_t):
        for i in blocks:
            keys = (i + 1) * ROWS
            r = slice(i * ROWS, keys)
            ok = allowed(self.first, i)
            for h in range(2):
                hs = slice(h * HEAD_DIM, (h + 1) * HEAD_DIM)
                scores = nn(self.k[0:keys], head_rows(self.q_t[:, r], h))
                prob = jnp.exp(jnp.where(ok, scores, MASKED) - self.lse[h : h + 1, r])
                centre = jnp.sum(da_t[hs, r].astype(F32) * self.o_t[hs, r], axis=0, keepdims=True)
                prob_grad = nn(self.v[0:keys], head_rows(da_t[:, r], h))
                score_grad = (prob * (prob_grad - centre)).astype(BF)
                dv[0:keys] += nn(prob.astype(BF), head_lanes(da[r], h))
                dk[0:keys] += nn(score_grad, head_lanes(self.q[r], h))
                dq_t[hs, r] = nn(self.k_t[hs, 0:keys], score_grad) * HEAD_DIM**-0.5

    def back_in(self, part, block, dk, dv, dq_t, proj_grad, cols, small, where_cols, where_small):
        r = span(block, ROWS)
        tables = self.tables[0][r], -self.tables[1][r], -self.tables[2][r]
        proj_grad[r, 0:128] = turned(dq_t[:, r].T, *tables).astype(BF)
        proj_grad[r, 128:256] = turned(dk[r], *tables).astype(BF)
        proj_grad[r, 256:384] = dv[r].astype(BF)
        pg, hg = proj_grad[r], self.slope[r]
        g1 = nt(pg, self.w[:, 0:384])
        g2 = nt(hg, self.w[:, 384:896])
        part[r] = (g1 * self.norms[0:1] + g2 * self.norms[1:2]).astype(BF)
        for grad, n, at in ((pg, 3, 0), (hg, 4, 3)):
            sums = jnp.sum(grad.astype(F32), axis=0, keepdims=True)
            for c in range(n):
                row = where_cols + at + c
                cols[row : row + 1] += sums[:, c * 128 : (c + 1) * 128]
        x = self.xg[r].astype(F32)
        for j, sums in enumerate((g1 * x, g2 * x, g1, g2)):
            row = where_small + j
            small[row : row + 1] += jnp.sum(sums, axis=0, keepdims=True)

    def grads(self, dw, gg, proj_grad, which):
        @pl.loop(0, 4)
        def _(j):
            c = span(j, ROWS)
            chips = pl.ds(j * 2, 2)

            def put(left, right, columns):
                dw[chips, :, :, columns] = nn(left, right).astype(BF).reshape(2, 2, 64, right.shape[1])

            x_t = self.xg[:, c].T.astype(F32)
            if "q" in which:
                n1_t = (x_t * self.norms_t[c, 0:1] + self.norms_t[c, 2:3]).astype(BF)
                put(n1_t, proj_grad[...], slice(0, 384))
            if "f" in which:
                n2_t = (x_t * self.norms_t[c, 1:2] + self.norms_t[c, 3:4]).astype(BF)
                put(n2_t, self.slope[...], slice(384, 896))
                put(gg[:, c].T, self.cat[...], slice(896, 1536))


INPUTS = (
    "tokens", "cotangent", "lengths", "frequency", "qkv_w", "in_w", "dense_w", "out_w",
    "gain", "shift", "qkv_b", "in_b", "dense_b", "out_b",
)
OUTPUTS = ("output", "input_grad", "dw_out", "qkv_b_grad", "in_b_grad", "bias_grad", "gain_grad", "shift_grad")


def scratch_list():
    n = 1024
    v = pltpu.VMEM
    items = {}
    for l in "01":
        items["xg" + l] = v((n, n), BF)
        items["gg" + l] = v((n, n), BF)
        items["w" + l] = v((n, 1536), BF)
        items["core_buf" + l] = v((8, 64, 1536), BF)
        items["chip_buf" + l] = v((7, 64, 1536), BF)
        for name in ("q", "k", "v"):
            items[name + l] = v((n, 128), BF)
        for name in ("q_t", "k_t"):
            items[name + l] = v((128, n), BF)
        items["o_t" + l] = v((128, n), F32)
        items["lse" + l] = v((8, n), F32)
        items["cat" + l] = v((n, 640), BF)
        items["slope" + l] = v((n, 512), BF)
        items["bs" + l] = DMA((2, 10))
        items["ts" + l] = DMA((2, 17))
        for name in ("fbuf", "bbuf"):
            items[name + l] = v((7, 128, n), BF)
    for l in ("q", "f", "1"):
        items["ws" + l] = DMA((2, 17))
        items["cs" + l] = DMA((2, 8))
    for l in "0ab":
        items["rs" + l] = DMA((2, 10))
        items["gs" + l] = DMA((2, 17))
    for l in ("1", "a", "b"):
        items["ds" + l] = DMA((2, 10))
        items["dc" + l] = DMA((2, 1))
    items["v_t"] = v((128, n), BF)
    items["part"] = v((n, n), BF)
    items["part_out"] = v((n, n), BF)
    items["dw"] = v((8, 2, 64, 1536), BF)
    items["mine"] = v((8, 64, 1536), BF)
    for name in ("cosine", "low", "high"):
        items[name] = v((n, 128), F32)
    items["first"] = v((1, n), jnp.int32)
    items["da"] = v((n, 128), BF)
    items["da_t"] = v((128, n), BF)
    items["proj_grad"] = v((n, 384), BF)
    items["dk"] = v((n, 128), F32)
    items["dv"] = v((n, 128), F32)
    items["dq_t"] = v((128, n), F32)
    items["stream1"] = v((128, n), F32)
    items["grad1"] = v((128, n), F32)
    items["small"] = v((16, n), F32)
    items["small_buf"] = v((7, 16, 128), F32)
    items["both"] = v((32, 128), F32)
    items["both_buf"] = v((15, 32, 128), F32)
    items["spread"] = v((8, 16, 128), F32)
    items["norms"] = v((2, 8, n), F32)
    items["norms_t"] = v((2, n, 8), F32)
    items["qkv_bias"] = v((2, 1, 384), F32)
    items["in_bias"] = v((2, 1, 512), F32)
    items["out_bias"] = v((2, n), F32)
    items["ss"] = DMA((2, 7))
    items["os"] = DMA((2, 15))
    items["es"] = DMA((2, 7))
    return items


DMA = pltpu.SemaphoreType.DMA


class Refs:
    pass


def whole_kernel(names, *refs):
    z = Refs()
    for name, ref in zip(names, refs):
        setattr(z, name, ref)
    d, t, core, tensor, chips = place()
    other = (d + 1 - 2 * core, t)
    mine_rows = span(t, 128)
    shard = span(d, 64)
    steps = [(r, p) for r in range(4) for p in range(2) if r or p]
    others = [(lax.rem(d + k, 16), t) for k in range(1, 16)]

    for l, w in enumerate((z.w0, z.w1)):
        for c in range(3):
            w[shard, c * 128 : (c + 1) * 128] = z.qkv_w[l, c]
        w[shard, 384:896] = z.in_w[l]
        w[shard, 896:1024] = z.dense_w[l]
        w[shard, 1024:1536] = z.out_w[l]
    z.xg0[mine_rows] = normed(z.tokens[...].astype(F32))[0].astype(BF)
    z.gg1[mine_rows] = z.cotangent[...]

    greet([tensor.device(*s) for s in steps] + others)
    rows0 = Gather(tensor, lambda i: z.xg0.at[span(i, 128)], 128, z.ts0)
    rows0.start()
    weights = {}
    for name, l, columns in (("q", 0, slice(0, 384)), ("f", 0, slice(384, 1536)), ("1", 1, slice(0, 1536))):
        dst = getattr(z, "w%d" % l)
        weights[name] = WeightGather(
            chips, other, core, columns, dst, getattr(z, "ws" + name), getattr(z, "cs" + name)
        )
    weights["q"].start()
    weights["f"].start()
    z.small[...] = jnp.zeros_like(z.small)
    z.both[...] = jnp.zeros_like(z.both)
    z.small[9:10] = jnp.sum(z.cotangent[...].astype(F32), axis=0, keepdims=True)
    for l in range(2):
        norms = jnp.concatenate([z.gain[l].astype(F32), z.shift[l].astype(F32)], axis=0)
        z.norms[l, 0:4] = norms
        z.norms_t[l] = z.norms[l].T
        for c in range(3):
            z.qkv_bias[l, 0:1, c * 128 : (c + 1) * 128] = z.qkv_b[c, l : l + 1].astype(F32)
    for l in range(2):
        z.in_bias[l] = z.in_b[l : l + 1].astype(F32)
    z.out_bias[...] = z.dense_b[...].astype(F32) + z.out_b[...].astype(F32)
    write_tables(z.lengths, z.frequency, z.cosine, z.low, z.high, z.first)
    rows0.middle()
    weights["q"].middle()
    weights["f"].middle()
    rows0.last()
    weights["q"].last()
    weights["f"].last()
    tables = (z.cosine, z.low, z.high)
    layers = [
        Layer(
            getattr(z, "xg%d" % l), getattr(z, "w%d" % l),
            z.norms.at[l], z.norms_t.at[l],
            z.qkv_bias.at[l], z.in_bias.at[l], tables, z.first,
            [getattr(z, "%s%d" % (name, l)) for name in KEPT],
        )
        for l in range(2)
    ]

    def blocks(*steps):
        return [lax.rem(tensor.ring + r, 4) for r in steps]

    weights["q"].finish()
    layers[0].project(z.v_t, blocks(0))
    rows0.near()
    layers[0].project(z.v_t, blocks(1, 3))
    rows0.far()

    def half_gather(h, sems):
        return Gather(tensor, lambda i: z.gg1.at[pl.ds(pl.multiple_of(i * 128 + h * 64, 64), 64)], 64, sems)

    cotangent = [half_gather(0, z.gsa), half_gather(1, z.gsb)]
    cotangent[0].start()

    def tensor_scatter(part, buf, sems):
        return Scatter(tensor, lambda i: part.at[span(i, 128)], lambda i: buf.at[i], 128, sems)

    def half_scatter(h, sems):
        rows = slice(h * 64, h * 64 + 64)
        return Scatter(
            tensor, lambda i: z.part_out.at[pl.ds(pl.multiple_of(i * 128 + h * 64, 64), 64)],
            lambda i: z.fbuf1.at[i, rows], 64, sems
        )

    layers[0].project(z.v_t, blocks(2))
    cotangent[0].middle()
    layers[0].attend(z.v_t)
    cotangent[0].last()
    weights["f"].finish()
    weights["1"].start()
    sum0 = tensor_scatter(z.part, z.fbuf0, z.rs0)
    for r in (2, 1, 3, 0):
        layers[0].branch(z.part, lax.rem(tensor.ring + r, 4))
        sum0.go(r)
    sum0.middle()
    sum0.last()
    weights["1"].middle()
    stream = z.tokens[...].astype(F32) + sum0.finish() + z.out_bias[0:1]
    z.stream1[...] = stream
    z.xg1[mine_rows] = normed(stream)[0].astype(BF)
    rows1 = Gather(tensor, lambda i: z.xg1.at[span(i, 128)], 128, z.ts1)
    rows1.start()
    weights["1"].last()
    rows1.middle()
    weights["1"].finish()
    layers[1].project(z.v_t, blocks(0))
    rows1.last()
    rows1.near()
    layers[1].project(z.v_t, blocks(1, 3))
    cotangent[0].finish()
    rows1.far()
    cotangent[1].start()

    layers[1].project(z.v_t, blocks(2))
    cotangent[1].middle()
    layers[1].attend(z.v_t)
    cotangent[1].last()
    sum1 = [half_scatter(0, z.rsa), half_scatter(1, z.rsb)]
    for r in (2, 1, 3, 0):
        layers[1].branch(z.part_out, lax.rem(tensor.ring + r, 4))
        sum1[0].go(r)

    def weight_scatter(tag, columns, l, sems, core_sems):
        return WeightScatter(
            chips, other, core, columns, z.dw, z.mine, getattr(z, "core_buf%d" % l),
            getattr(z, "chip_buf%d" % l), sems, core_sems,
        )

    z.dk[...] = jnp.zeros_like(z.dk)
    z.dv[...] = jnp.zeros_like(z.dv)
    cotangent[1].finish()
    layers[1].back_out(z.gg1, z.da, z.da_t, blocks(0, 1, 3, 2))
    layers[1].attend_back((0, 1), z.da, z.da_t, z.dk, z.dv, z.dq_t)
    sum1[0].middle()
    layers[1].attend_back((2, 3), z.da, z.da_t, z.dk, z.dv, z.dq_t)
    sum1[0].last()
    back1 = tensor_scatter(z.part, z.bbuf1, z.bs1)
    for r in (2, 1, 3, 0):
        layers[1].back_in(
            z.part, lax.rem(tensor.ring + r, 4), z.dk, z.dv, z.dq_t, z.proj_grad, z.both, z.small, 23, 4
        )
        back1.go(r)
    layers[1].grads(z.dw, z.gg1, z.proj_grad, "f")
    back1.middle()
    layers[1].grads(z.dw, z.gg1, z.proj_grad, "q")
    weights_back1 = weight_scatter("1", slice(0, 1536), 1, z.ds1, z.dc1)
    weights_back1.start()
    back1.last()
    grad = stream_back(back1.finish(), z.cotangent[...].astype(F32), z.stream1[...])
    z.grad1[...] = grad
    z.gg0[mine_rows] = grad.astype(BF)
    grads0 = Gather(tensor, lambda i: z.gg0.at[span(i, 128)], 128, z.gs0)
    grads0.start()
    weights_back1.spread()
    z.small[8:9] = jnp.sum(grad, axis=0, keepdims=True)
    z.dk[...] = jnp.zeros_like(z.dk)
    z.dv[...] = jnp.zeros_like(z.dv)
    grads0.middle()
    layers[0].back_out(z.gg0, z.da, z.da_t, blocks(0))
    grads0.last()
    weights_back1.middle()
    z.output[0:64] = (z.stream1[0:64] + sum1[0].finish() + z.out_bias[1:2]).astype(BF)
    grads0.near()
    layers[0].back_out(z.gg0, z.da, z.da_t, blocks(1, 3))
    grads0.far()
    for r in (2, 1, 3):
        sum1[1].go(r)

    layers[0].back_out(z.gg0, z.da, z.da_t, blocks(2))
    weights_back1.last()
    layers[0].grads(z.dw, z.gg0, z.proj_grad, "f")
    weights_back0 = weight_scatter("a", slice(384, 1536), 0, z.dsa, z.dca)
    weights_back0.start()
    layers[0].attend_back((0, 1), z.da, z.da_t, z.dk, z.dv, z.dq_t)
    z.dw_out[1] = weights_back1.finish()
    weights_back0.spread()
    sum1[1].middle()
    layers[0].attend_back((2, 3), z.da, z.da_t, z.dk, z.dv, z.dq_t)
    sum1[1].last()
    back0 = tensor_scatter(z.part, z.bbuf0, z.bs0)
    for r in (2, 1, 3, 0):
        layers[0].back_in(
            z.part, lax.rem(tensor.ring + r, 4), z.dk, z.dv, z.dq_t, z.proj_grad, z.both, z.small, 16, 0
        )
        back0.go(r)
    small = [
        send(z.small.at[:, span(tensor.block(*s), 128)], z.small_buf.at[i], z.ss, i, tensor.device(*s))
        for i, s in enumerate(steps)
    ]
    layers[0].grads(z.dw, z.gg0, z.proj_grad, "q")
    weights_last = weight_scatter("b", slice(0, 384), 0, z.dsb, z.dcb)
    weights_last.start()
    weights_back0.middle()
    back0.middle()
    weights_last.spread()
    weights_back0.last()
    back0.last()
    for c in small:
        c.wait()
    total = z.small[:, span(t, 128)]
    for i in range(7):
        total = total + z.small_buf[i]
    z.both[0:16] = total
    both = [send(z.both, z.both_buf.at[i], z.os, i, p) for i, p in enumerate(others)]
    weights_last.middle()
    weights_last.last()
    for c in both:
        c.wait()
    total = z.both[...]
    for i in range(15):
        total = total + z.both_buf[i]
    z.spread[t] = total[0:16]
    spread = [
        send(z.spread.at[t], z.spread.at[t], z.es, i, tensor.device(*s)) for i, s in enumerate(steps)
    ]
    for l in range(2):
        for c in range(3):
            row = 16 + 7 * l + c
            z.qkv_b_grad[c, l : l + 1] = total[row : row + 1]
        for c in range(4):
            row = 19 + 7 * l + c
            z.in_b_grad[l : l + 1, c * 128 : (c + 1) * 128] = total[row : row + 1]
    z.output[64:128] = (z.stream1[64:128] + sum1[1].finish() + z.out_bias[1:2]).astype(BF)
    z.dw_out[0, :, 384:1536] = weights_back0.finish()
    z.input_grad[...] = stream_back(back0.finish(), z.grad1[...], z.tokens[...].astype(F32))
    z.dw_out[0, :, 0:384] = weights_last.finish()
    for c in spread:
        c.wait()
    for i in range(8):
        lanes = slice(i * 128, (i + 1) * 128)
        for l in range(2):
            z.gain_grad[l, :, lanes] = z.spread[i, 4 * l : 4 * l + 2]
            z.shift_grad[l, :, lanes] = z.spread[i, 4 * l + 2 : 4 * l + 4]
        z.bias_grad[:, lanes] = z.spread[i, 8:10]


def result_kernel(
    output, input_grad, dw, qkv_b_grad, in_b_grad, bias_grad, gain_grad, shift_grad,
    output_to, input_grad_to, qkv_to, qkv_b_to, dense_to, dense_b_to, in_to, in_b_to, out_to, out_b_to,
    gain_to, shift_to,
):
    output_to[...] = output[...]
    input_grad_to[...] = input_grad[...]
    for l in range(2):
        for c in range(3):
            qkv_to[l, c] = dw[l, :, c * 128 : (c + 1) * 128]
        in_to[l] = dw[l, :, 384:896]
        dense_to[l] = dw[l, :, 896:1024]
        out_to[l] = dw[l, :, 1024:1536]
    qkv_b_to[...] = qkv_b_grad[...]
    in_b_to[...] = in_b_grad[...]
    dense_b_to[...] = bias_grad[...]
    out_b_to[...] = bias_grad[...]
    gain_to[...] = gain_grad[...]
    shift_to[...] = shift_grad[...]


def local(
    tokens,
    lengths,
    qkv_weight,
    qkv_bias,
    dense_weight,
    dense_bias,
    fc_in_weight,
    fc_in_bias,
    fc_out_weight,
    fc_out_bias,
    norm_gain,
    norm_bias,
    cotangent,
):
    lane = np.arange(128) % HEAD_DIM
    half_rot = ROT // 2
    frequency = np.where(lane < ROT, 10000.0 ** (-(2.0 * (lane % half_rot)) / ROT), 0.0)
    inputs = (
        tokens,
        cotangent,
        lengths,
        jnp.asarray(frequency[None, :], F32),
        qkv_weight.swapaxes(1, 2),
        fc_in_weight,
        dense_weight.swapaxes(1, 2),
        fc_out_weight.swapaxes(1, 2),
        norm_gain,
        norm_bias,
        qkv_bias.swapaxes(0, 1),
        fc_in_bias,
        dense_bias,
        fc_out_bias,
    )
    s = jax.ShapeDtypeStruct
    shapes = (
        s((128, 1024), BF),
        s((128, 1024), F32),
        s((2, 64, 1536), F32),
        s((3, 2, 128), F32),
        s((2, 512), F32),
        s((2, 1024), F32),
        s((2, 2, 1024), F32),
        s((2, 2, 1024), F32),
    )
    scratch = scratch_list()
    names = INPUTS + OUTPUTS + tuple(scratch)
    results = pl.pallas_call(
        lambda *refs: whole_kernel(names, *refs),
        out_shape=shapes,
        in_specs=[VM] * len(inputs),
        out_specs=(VM,) * len(shapes),
        scratch_shapes=list(scratch.values()),
        compiler_params=pltpu.CompilerParams(
            collective_id=1, has_side_effects=True, vmem_limit_bytes=63 * 2**20
        ),
        cost_estimate=pl.CostEstimate(flops=0, bytes_accessed=600_000_000, transcendentals=0),
        name="layers_forward_and_backward",
    )(*inputs)
    shapes = (
        s((128, 1024), BF),
        s((128, 1024), F32),
        s((2, 3, 64, 128), F32),
        s((3, 2, 128), F32),
        s((2, 64, 128), F32),
        s((2, 1024), F32),
        s((2, 64, 512), F32),
        s((2, 512), F32),
        s((2, 64, 512), F32),
        s((2, 1024), F32),
        s((2, 2, 1024), F32),
        s((2, 2, 1024), F32),
    )
    final = pl.pallas_call(
        result_kernel,
        out_shape=shapes,
        in_specs=[VM] * len(results),
        out_specs=(VM,) * len(shapes),
        compiler_params=pltpu.CompilerParams(vmem_limit_bytes=60 * 2**20),
        cost_estimate=pl.CostEstimate(flops=0, bytes_accessed=6_000_000, transcendentals=0),
        name="results",
    )(*results)
    output, input_grad, qkv, qkv_b, dense, dense_b, fc_in, fc_in_b, fc_out, fc_out_b, gains, shifts = final
    return (
        output,
        input_grad,
        qkv.swapaxes(1, 2),
        qkv_b.swapaxes(0, 1),
        dense.swapaxes(1, 2),
        dense_b,
        fc_in,
        fc_in_b,
        fc_out.swapaxes(1, 2),
        fc_out_b,
        gains,
        shifts,
    )


def solution(mesh):
    return jax.shard_map(
        local,
        mesh=mesh,
        in_specs=(
            P(("dp", "tensor"), None),
            P("dp", None),
            P(None, "dp", None, "tensor"),
            P(None, None, "tensor"),
            P(None, "tensor", "dp"),
            P(),
            P(None, "dp", "tensor"),
            P(None, "tensor"),
            P(None, "tensor", "dp"),
            P(),
            P(),
            P(),
            P(("dp", "tensor"), None),
        ),
        out_specs=(
            P(("dp", "tensor"), None),
            P(("dp", "tensor"), None),
            P(None, "dp", None, "tensor"),
            P(None, None, "tensor"),
            P(None, "tensor", "dp"),
            P(),
            P(None, "dp", "tensor"),
            P(None, "tensor"),
            P(None, "tensor", "dp"),
            P(),
            P(),
            P(),
        ),
        check_vma=False,
    )
```
